32 devices in a mesh: ctx: 8 (over z, y), fft: 4 (over x, core).
Axes of the slice: x: 2, y: 2, z: 4, core: 2. Of those that a mesh axis runs over, the one named last changes fastest.
Arguments:
- streams: bfloat16 [3, 1024, 2048], P(None, 'ctx', 'fft'), may hold values from -6 to 6
- taps: float32 [3, 7, 2048], P(None, None, 'fft'), may hold values from -2 to 2
- filters: bfloat16 [1024, 2048], P('ctx', 'fft')
- cotangent: bfloat16 [1024, 2048], P('ctx', 'fft')
Outputs:
- gated: bfloat16 [1024, 2048], P('ctx', 'fft')
- stream_grad: bfloat16 [3, 1024, 2048], P(None, 'ctx', 'fft')
- filter_grad: bfloat16 [1024, 2048], P('ctx', 'fft')
- tap_grad: float32 [3, 7, 2048], P(None, None, 'fft')
The draws below stay inside these ranges and needn't reach their ends.
All inputs are finite; a program needn't handle non-finite values.
Results may differ from the reference program's by a relative error of at most 0.012.
Values may be sent and summed in bfloat16 or wider, within the bound.
No kernel may reach another device: no remote copies, remote signals or barrier semaphores. Data moves between devices by JAX's collectives and lax.ppermute only.
A program may use at most 64 MiB of HBM per device.

```python
import math
import jax
import jax.numpy as jnp
from jax import lax

CH = 2048
TAPS = 7
SEQ = 1024


def draw_filters(key, part):
    scale_factor = SEQ ** (-0.5)
    values = jnp.clip(jax.random.normal(key, (SEQ, CH), jnp.float32), -4.0, 4.0) * scale_factor
    return values.astype(jnp.bfloat16)


def draw_cotangent(key, part):
    position = jnp.arange(SEQ, dtype=jnp.float32)[:, None] / (SEQ - 1)
    noise_part = jnp.clip(jax.random.normal(key, (SEQ, CH), jnp.float32), -4.0, 4.0)
    growth = 1.0 + 2.0 * position
    return (noise_part * growth).astype(jnp.bfloat16)


def block_scale(stream_key, shape, cuts, smallest, high):
    factor_of = 1.0
    for dim, blocks in cuts:
        steps = jax.random.uniform(jax.random.fold_in(jax.random.fold_in(stream_key, 6), dim), (blocks,), jnp.float32, smallest / len(cuts), high / len(cuts))
        factor_of = factor_of * jnp.repeat(jnp.exp(steps), shape[dim] // blocks).reshape((-1,) + (1,) * (len(shape) - 1 - dim))
    return factor_of


def centred(key, extent, width, bound, cuts=(), held_as=jnp.bfloat16):
    drawn = width * jax.random.normal(key, extent, jnp.float32)
    if cuts:
        drawn = drawn * block_scale(key, extent, cuts, -0.22, 0.18)
    return jnp.clip(drawn, -bound, bound).astype(held_as)


def setup_inputs(seed: int = 0) -> dict:
    streams_of = jax.random.split(jax.random.key(seed), 5)
    streams = centred(streams_of[0], (3, SEQ, CH), 1.0, 6.0, ((1, 8), (2, 4)))
    taps = centred(streams_of[1], (3, TAPS, CH), TAPS ** -0.5, 2.0, ((2, 4),), jnp.float32)
    filters = draw_filters(jax.random.fold_in(streams_of[4], 71), 0)
    cotangent = draw_cotangent(jax.random.fold_in(streams_of[4], 71), 0)
    return dict(streams=streams, taps=taps, filters=filters, cotangent=cotangent)


def short_conv(streams, taps):
    tap_reach = taps.shape[1] - 1
    widened = jnp.pad(streams.astype(jnp.float32), ((0, 0), (tap_reach, 0), (0, 0)))
    running = jnp.zeros((3, SEQ, CH), jnp.float32)
    for offset in range(tap_reach + 1):
        running = running + taps[:, offset, None, :].astype(jnp.float32) * widened[:, tap_reach - offset:tap_reach - offset + SEQ, :]
    return (running, widened)

def spectrum(values):
    return jnp.fft.rfft(values.astype(jnp.float32), n=2 * SEQ, axis=0)

def inverse_spectrum(spec):
    return jnp.fft.irfft(spec, n=2 * SEQ, axis=0)[:SEQ]

def reference(streams, taps, filters, cotangent):
    convolved, widened = short_conv(streams, taps)
    query_side = convolved[0]
    key_side = convolved[1]
    value_side = convolved[2]
    product = (key_side * value_side).astype(jnp.bfloat16)
    product_spec = spectrum(product)
    filter_spec = spectrum(filters)
    mixed = inverse_spectrum(product_spec * filter_spec).astype(jnp.bfloat16)
    mixed_wide = mixed.astype(jnp.float32)
    gated = (query_side * mixed_wide).astype(jnp.bfloat16)
    upstream = cotangent.astype(jnp.float32)
    mixed_grad = (upstream * query_side).astype(jnp.bfloat16)
    query_grad = upstream * mixed_wide
    grad_spec = spectrum(mixed_grad)
    product_grad = inverse_spectrum(jnp.conj(filter_spec) * grad_spec).astype(jnp.bfloat16)
    scale_factor = 1.0 / math.sqrt(SEQ)
    filter_grad = (inverse_spectrum(jnp.conj(product_spec) * grad_spec) * scale_factor).astype(jnp.bfloat16)
    product_wide = product_grad.astype(jnp.float32)
    conv_grad = jnp.stack([query_grad, product_wide * value_side, product_wide * key_side])
    tap_reach = taps.shape[1] - 1
    extended_grad = jnp.pad(conv_grad, ((0, 0), (0, tap_reach), (0, 0)))
    running = jnp.zeros((3, SEQ, CH), jnp.float32)
    for offset in range(tap_reach + 1):
        running = running + taps[:, offset, None, :].astype(jnp.float32) * extended_grad[:, offset:offset + SEQ, :]
    stream_grad = running.astype(jnp.bfloat16)
    tap_terms = jnp.stack([lax.optimization_barrier(jnp.sum(conv_grad * widened[:, tap_reach - offset:tap_reach - offset + SEQ, :], axis=1)) for offset in range(tap_reach + 1)], axis=1)
    tap_grad = tap_terms * scale_factor
    return (gated, stream_grad, filter_grad, tap_grad)
```

```python
import functools
import math

import jax
import jax.numpy as jnp
import numpy as np
from jax import lax
from jax.experimental import pallas as pl
from jax.experimental.pallas import tpu as pltpu
from jax.sharding import PartitionSpec as P

exact_mode = lax.Precision.HIGHEST
LANES = 128
HALF = LANES // 2
EDGE = 8
TAP_ROWS = 32
TABLE_BYTES = 16 * 1024 * 1024
VMEM_BYTES = 48 * 1024 * 1024


def odd_tables(total):
    freq = 2 * np.arange(total)[:, None] + 1
    angles = (freq * np.arange(total)[None, :] % (4 * total)) * (math.pi / (2 * total))
    table = np.concatenate([np.cos(angles), -np.sin(angles)])
    high = table.astype(jnp.bfloat16)
    back = np.ascontiguousarray(table.T / total).astype(jnp.bfloat16)
    return high, back


def lower_lanes(rows):
    return lax.broadcasted_iota(jnp.int32, (rows, LANES), 1) < HALF


def turned(value):
    return pltpu.roll(value, HALF, 1)


def wide(value):
    return value.astype(jnp.float32)


def paired(first, second, odd, low):
    left = jnp.where(odd, turned(first), first)
    right = jnp.where(odd, second, turned(second))
    return jnp.where(low, left, right).astype(jnp.bfloat16)


def pack_kernel(count, streams_ref, filters_ref, cotangent_ref, taps_ref, *out_refs):
    me = lax.axis_index("ctx")
    rows = filters_ref.shape[0]
    half_rows = rows // 2
    tap_count = taps_ref.shape[1]
    low = lower_lanes(rows)
    low_half = lower_lanes(half_rows)
    for step in range(count):
        owner = lax.rem(me + step, count)
        cols = pl.ds(pl.multiple_of(owner // 2 * LANES, LANES), LANES)
        odd = lax.rem(owner, 2) == 1
        out = out_refs[step]
        out[0:rows, :] = paired(wide(streams_ref[1, :, cols]), wide(streams_ref[2, :, cols]), odd, low)
        out[rows : 2 * rows, :] = paired(wide(streams_ref[0, :, cols]), wide(cotangent_ref[:, cols]), odd, low)
        lag_block = wide(filters_ref[:, cols])
        out[2 * rows :, :] = paired(lag_block[:half_rows], lag_block[half_rows:], odd, low_half)
    cols = pl.ds(pl.multiple_of(me // 2 * LANES, LANES), LANES)
    odd = lax.rem(me, 2) == 1
    tap_out = out_refs[count]
    low_taps = lower_lanes(tap_count)
    here = [jnp.where(odd, turned(taps_ref[i, :, cols]), taps_ref[i, :, cols]) for i in range(3)]
    first_tap = lax.broadcasted_iota(jnp.int32, (tap_count, LANES), 0) == 0
    tap_out[...] = jnp.zeros_like(tap_out)
    tap_out[0:tap_count, :] = jnp.where(low_taps, here[1], turned(here[2]))
    tap_out[EDGE : EDGE + tap_count, :] = jnp.where(low_taps, here[0], jnp.where(first_tap, 1.0, 0.0))


def main_kernel(count, tap_count, scale, *refs):
    in_refs = refs[:count]
    tap_ref, table_hbm, back_hbm = refs[count : count + 3]
    out_refs = refs[count + 3 : 2 * count + 3]
    (raw_kv, raw_qc, conv_kv, conv_qc, signals, spectra, grad_kv, grad_q, lag_grad,
     table, back, sems) = refs[2 * count + 3 :]
    me = lax.axis_index("ctx")
    total = signals.shape[0]
    rows = total // count
    half_rows = rows // 2
    low = lower_lanes(rows)
    low_half = lower_lanes(half_rows)
    table_copy = pltpu.make_async_copy(table_hbm, table, sems.at[0])
    back_copy = pltpu.make_async_copy(back_hbm, back, sems.at[1])
    table_copy.start()
    back_copy.start()

    raw_kv[0:EDGE, :] = jnp.zeros((EDGE, LANES), jnp.float32)
    raw_qc[0:EDGE, :] = jnp.zeros((EDGE, LANES), jnp.float32)
    grad_kv[total:, :] = jnp.zeros((EDGE, LANES), jnp.float32)
    grad_q[total:, :] = jnp.zeros((EDGE, LANES), jnp.float32)
    for step in range(count):
        source = lax.rem(me - step + count, count)
        base = pl.multiple_of(source * rows, rows)
        block = in_refs[step]
        raw_kv[pl.ds(base + EDGE, rows), :] = wide(block[0:rows, :])
        raw_qc[pl.ds(base + EDGE, rows), :] = wide(block[rows : 2 * rows, :])
        lag_block = wide(block[2 * rows :, :])
        other = turned(lag_block)
        signals[pl.ds(base, half_rows), LANES:] = jnp.where(low_half, lag_block, other).astype(jnp.bfloat16)
        signals[pl.ds(base + half_rows, half_rows), LANES:] = jnp.where(low_half, other, lag_block).astype(jnp.bfloat16)

    tap_kv = [tap_ref[j : j + 1, :] for j in range(tap_count)]
    tap_q = [tap_ref[EDGE + j : EDGE + j + 1, :] for j in range(tap_count)]

    for block in range(count):
        base = block * rows
        key_value = jnp.zeros((rows, LANES), jnp.float32)
        query_cot = jnp.zeros((rows, LANES), jnp.float32)
        for j in range(tap_count):
            window = slice(base + EDGE - j, base + EDGE - j + rows)
            key_value = key_value + tap_kv[j] * raw_kv[window, :]
            query_cot = query_cot + tap_q[j] * raw_qc[window, :]
        conv_kv[base : base + rows, :] = key_value
        conv_qc[base : base + rows, :] = query_cot
        product = key_value * turned(key_value)
        mixed_grad = query_cot * turned(query_cot)
        signals[base : base + rows, :LANES] = jnp.where(low, product, mixed_grad).astype(jnp.bfloat16)

    table_copy.wait()
    part = min(256, total)
    low_part = lower_lanes(part)
    for start in range(0, total, part):
        real = jnp.dot(table[start : start + part, :], signals[...], preferred_element_type=jnp.float32)
        imag = jnp.dot(
            table[total + start : total + start + part, :], signals[...], preferred_element_type=jnp.float32
        )
        a_re, b_re = real[:, :LANES], real[:, LANES:]
        a_im, b_im = imag[:, :LANES], imag[:, LANES:]
        b_im = jnp.where(low_part, b_im, -b_im)
        r_re, r_im = turned(a_re), turned(a_im)
        spectra[start : start + part, :LANES] = (a_re * b_re - a_im * b_im).astype(jnp.bfloat16)
        spectra[start : start + part, LANES:] = (a_re * r_re + a_im * r_im).astype(jnp.bfloat16)
        spectra[total + start : total + start + part, :LANES] = (a_re * b_im + a_im * b_re).astype(jnp.bfloat16)
        spectra[total + start : total + start + part, LANES:] = (a_re * r_im - a_im * r_re).astype(jnp.bfloat16)

    back_copy.wait()
    for block in range(count):
        base = block * rows
        here = slice(base, base + rows)
        result = jnp.dot(back[here, :], spectra[...], preferred_element_type=jnp.float32)
        pair = wide(result[:, :LANES].astype(jnp.bfloat16))
        other = turned(pair)
        gated_grad = conv_qc[here, :] * jnp.where(low, pair, other)
        grad_q[here, :] = turned(gated_grad)
        grad_kv[here, :] = jnp.where(low, other, pair) * turned(conv_kv[here, :])
        lag_terms = result[:, LANES:] * scale
        lag_grad[block * half_rows : (block + 1) * half_rows, :] = jnp.where(
            low_half, lag_terms[:half_rows], turned(lag_terms[half_rows:])
        )

    tap_sum_kv = [jnp.zeros((EDGE, LANES), jnp.float32)] * tap_count
    tap_sum_q = [jnp.zeros((EDGE, LANES), jnp.float32)] * tap_count
    for step in range(count):
        owner = lax.rem(me + step, count)
        base = pl.multiple_of(owner * rows, rows)
        out = out_refs[step]
        stream_kv = jnp.zeros((rows, LANES), jnp.float32)
        stream_q = jnp.zeros((rows, LANES), jnp.float32)
        for j in range(tap_count):
            stream_kv = stream_kv + tap_kv[j] * grad_kv[pl.ds(base + j, rows), :]
            stream_q = stream_q + tap_q[j] * grad_q[pl.ds(base + j, rows), :]
        out[0:rows, :] = stream_kv.astype(jnp.bfloat16)
        out[rows : 2 * rows, :] = stream_q.astype(jnp.bfloat16)
        lag_base = pl.multiple_of(owner * half_rows, half_rows)
        out[2 * rows : 2 * rows + half_rows, :] = lag_grad[pl.ds(lag_base, half_rows), :].astype(jnp.bfloat16)
    for block in range(count):
        base = block * rows
        kv = grad_kv[base : base + rows, :]
        q = grad_q[base : base + rows, :]
        for j in range(tap_count):
            window = slice(base + EDGE - j, base + EDGE - j + rows)
            tap_sum_kv[j] = tap_sum_kv[j] + jnp.sum((kv * raw_kv[window, :]).reshape(rows // EDGE, EDGE, LANES), axis=0)
            tap_sum_q[j] = tap_sum_q[j] + jnp.sum((q * raw_qc[window, :]).reshape(rows // EDGE, EDGE, LANES), axis=0)
    spare = [jnp.zeros((1, LANES), jnp.float32)] * (EDGE - tap_count)
    sums = jnp.concatenate(
        [jnp.sum(s, axis=0, keepdims=True) for s in tap_sum_kv] + spare
        + [jnp.sum(s, axis=0, keepdims=True) for s in tap_sum_q] + spare, axis=0
    ) * scale
    high = sums.astype(jnp.bfloat16)
    both = jnp.concatenate([wide(high), sums - wide(high)], axis=0).astype(jnp.bfloat16)
    for step in range(count):
        out_refs[step][2 * rows + half_rows :, :] = both


def unpack_kernel(count, tap_count, *refs):
    in_refs = refs[:count]
    gated_ref, stream_ref, lag_ref, tap_ref = refs[count : count + 4]
    blocks = refs[count + 4]
    me = lax.axis_index("ctx")
    rows = gated_ref.shape[0]
    half_rows = rows // 2
    low = lower_lanes(rows)
    low_half = lower_lanes(half_rows)
    low_taps = lower_lanes(EDGE)
    for step in range(count):
        owner = lax.rem(me - step + count, count)
        blocks[owner, :, :] = in_refs[step][...]
    for pair in range(count // 2):
        cols = slice(pair * LANES, (pair + 1) * LANES)
        even, odd = wide(blocks[2 * pair, :, :]), wide(blocks[2 * pair + 1, :, :])
        turned_even, turned_odd = turned(even), turned(odd)

        def lower_of(window, mask):
            return jnp.where(mask, even[window], turned_odd[window])

        def upper_of(window, mask):
            return jnp.where(mask, turned_even[window], odd[window])

        key_value, query_gated = slice(0, rows), slice(rows, 2 * rows)
        stream_ref[1, :, cols] = lower_of(key_value, low).astype(jnp.bfloat16)
        stream_ref[2, :, cols] = upper_of(key_value, low).astype(jnp.bfloat16)
        stream_ref[0, :, cols] = lower_of(query_gated, low).astype(jnp.bfloat16)
        gated_ref[:, cols] = upper_of(query_gated, low).astype(jnp.bfloat16)
        lags = slice(2 * rows, 2 * rows + half_rows)
        lag_ref[0:half_rows, cols] = lower_of(lags, low_half).astype(jnp.bfloat16)
        lag_ref[half_rows:, cols] = upper_of(lags, low_half).astype(jnp.bfloat16)
        start = 2 * rows + half_rows
        high_kv, high_q, rest_kv, rest_q = [slice(start + g * EDGE, start + (g + 1) * EDGE) for g in range(4)]
        tap_ref[1, :, cols] = (lower_of(high_kv, low_taps) + lower_of(rest_kv, low_taps))[:tap_count]
        tap_ref[2, :, cols] = (upper_of(high_kv, low_taps) + upper_of(rest_kv, low_taps))[:tap_count]
        tap_ref[0, :, cols] = (lower_of(high_q, low_taps) + lower_of(rest_q, low_taps))[:tap_count]


def exchanged(blocks):
    count = len(blocks)
    return [blocks[0]] + [
        lax.ppermute(blocks[step], "ctx", [(source, (source + step) % count) for source in range(count)])
        for step in range(1, count)
    ]


def in_vmem(count):
    return [pl.BlockSpec(memory_space=pltpu.VMEM)] * count


def local_dense(streams, taps, filters, cotangent):
    count = lax.axis_size("ctx")
    rows, channels = filters.shape
    tap_count = taps.shape[1]
    total = rows * count
    params = pltpu.CompilerParams(vmem_limit_bytes=VMEM_BYTES)
    sent_rows = 2 * rows + rows // 2
    packed = pl.pallas_call(
        functools.partial(pack_kernel, count),
        out_shape=[jax.ShapeDtypeStruct((sent_rows, LANES), jnp.bfloat16)] * count
        + [jax.ShapeDtypeStruct((2 * EDGE, LANES), jnp.float32)],
        in_specs=in_vmem(4),
        out_specs=in_vmem(count + 1),
        compiler_params=params,
        name="pack",
    )(streams, filters, cotangent, taps)
    arrived = exchanged(packed[:count])
    table, back = odd_tables(total)
    back_rows = sent_rows + TAP_ROWS
    f32_rows = lambda extent: pltpu.VMEM((extent, LANES), jnp.float32)
    made = pl.pallas_call(
        functools.partial(main_kernel, count, tap_count, 1.0 / math.sqrt(total)),
        out_shape=[jax.ShapeDtypeStruct((back_rows, LANES), jnp.bfloat16)] * count,
        in_specs=in_vmem(count + 1) + [pl.BlockSpec(memory_space=pl.ANY)] * 2,
        out_specs=in_vmem(count),
        scratch_shapes=[
            f32_rows(total + EDGE), f32_rows(total + EDGE), f32_rows(total), f32_rows(total),
            pltpu.VMEM((total, 2 * LANES), jnp.bfloat16), pltpu.VMEM((2 * total, 2 * LANES), jnp.bfloat16),
            f32_rows(total + EDGE), f32_rows(total + EDGE), f32_rows(total // 2),
            pltpu.VMEM(table.shape, jnp.bfloat16), pltpu.VMEM(back.shape, jnp.bfloat16),
            pltpu.SemaphoreType.DMA((2,)),
        ],
        compiler_params=params,
        name="channels",
    )(*arrived, packed[count], jnp.asarray(table), jnp.asarray(back))
    returned = exchanged(made)
    return tuple(
        pl.pallas_call(
            functools.partial(unpack_kernel, count, tap_count),
            out_shape=[
                jax.ShapeDtypeStruct(filters.shape, jnp.bfloat16),
                jax.ShapeDtypeStruct(streams.shape, jnp.bfloat16),
                jax.ShapeDtypeStruct(filters.shape, jnp.bfloat16),
                jax.ShapeDtypeStruct(taps.shape, jnp.float32),
            ],
            in_specs=in_vmem(count),
            out_specs=in_vmem(4),
            scratch_shapes=[pltpu.VMEM((count, back_rows, LANES), jnp.bfloat16)],
            compiler_params=params,
            name="unpack",
        )(*returned)
    )


def shifted(value, axis, steps):
    count = lax.axis_size(axis)
    first, last = (max(0, -steps), min(count, count - steps))
    return lax.ppermute(value, axis, [(source, source + steps) for source in range(first, last)])


def angle_table(row_count, col_count, col_start, period):
    row_ids = lax.iota(jnp.int32, row_count)
    col_ids = col_start + lax.iota(jnp.int32, col_count)
    turns = row_ids[:, None] * col_ids[None, :] % period
    angles = turns.astype(jnp.float32) * (2.0 * math.pi / period)
    return (jnp.cos(angles), jnp.sin(angles))


def column_start():
    return 0


def split_product(table, signal):
    high_part = table.astype(jnp.bfloat16)
    low_part = (table - high_part.astype(jnp.float32)).astype(jnp.bfloat16)
    first = jnp.einsum("kt,ctu->cku", high_part, signal, preferred_element_type=jnp.float32)
    second = jnp.einsum("kt,ctu->cku", low_part, signal, preferred_element_type=jnp.float32)
    return first + second


def forward_transform(signal):
    input_rows = signal.shape[1]
    row_count = 2 * input_rows
    col_count = signal.shape[2]
    period = row_count * col_count
    cos_first, sin_first = angle_table(row_count, input_rows, 0, row_count)
    first_re = split_product(cos_first, signal)
    first_im = -split_product(sin_first, signal)
    cos_twist, sin_twist = angle_table(row_count, col_count, column_start(), period)
    turned_re = first_re * cos_twist + first_im * sin_twist
    turned_im = first_im * cos_twist - first_re * sin_twist
    cos_second, sin_second = angle_table(col_count, col_count, 0, col_count)
    spec_re = jnp.einsum("cut,tk->cuk", turned_re, cos_second, precision=exact_mode) + jnp.einsum(
        "cut,tk->cuk", turned_im, sin_second, precision=exact_mode
    )
    spec_im = jnp.einsum("cut,tk->cuk", turned_im, cos_second, precision=exact_mode) - jnp.einsum(
        "cut,tk->cuk", turned_re, sin_second, precision=exact_mode
    )
    return (spec_re, spec_im)


def inverse_transform(spec_re, spec_im, keep_rows):
    full_width = spec_re.shape[2]
    cos_second, sin_second = angle_table(full_width, full_width, 0, full_width)
    back_re = jnp.einsum("cuk,kt->cut", spec_re, cos_second, precision=exact_mode) - jnp.einsum(
        "cuk,kt->cut", spec_im, sin_second, precision=exact_mode
    )
    back_im = jnp.einsum("cuk,kt->cut", spec_im, cos_second, precision=exact_mode) + jnp.einsum(
        "cuk,kt->cut", spec_re, sin_second, precision=exact_mode
    )
    row_count = back_re.shape[1]
    col_count = back_re.shape[2]
    period = row_count * full_width
    cos_twist, sin_twist = angle_table(row_count, col_count, column_start(), period)
    turned_re = back_re * cos_twist - back_im * sin_twist
    turned_im = back_im * cos_twist + back_re * sin_twist
    cos_first, sin_first = angle_table(keep_rows, row_count, 0, row_count)
    result = jnp.einsum("tk,cku->ctu", cos_first, turned_re, precision=exact_mode) - jnp.einsum(
        "tk,cku->ctu", sin_first, turned_im, precision=exact_mode
    )
    return result * (1.0 / period)


def regroup_out(stacked):
    count_here = stacked.shape[0]
    channel_count = stacked.shape[1]
    block_rows = stacked.shape[2]
    shaped = stacked.reshape(count_here, channel_count, 1, block_rows)
    return lax.all_to_all(shaped, "ctx", split_axis=1, concat_axis=2, tiled=True)


def regroup_back(stacked):
    count_here = stacked.shape[0]
    arrived = lax.all_to_all(stacked, "ctx", split_axis=2, concat_axis=1, tiled=True)
    return arrived.reshape(count_here, arrived.shape[1], arrived.shape[3])


def merged(block):
    return block.reshape(block.shape[0] * block.shape[1], block.shape[2], block.shape[3])


def local_factored(streams, taps, filters, cotangent):
    block_rows = streams.shape[1]
    tap_reach = taps.shape[1] - 1
    earlier = shifted(streams[:, block_rows - tap_reach :, :], "ctx", 1)
    extended = jnp.concatenate([earlier, streams], axis=1).astype(jnp.float32)
    convolved = jnp.zeros((3, block_rows, streams.shape[2]), jnp.float32)
    for offset in range(tap_reach + 1):
        convolved = (
            convolved
            + taps[:, offset, None, :]
            * extended[:, tap_reach - offset : tap_reach - offset + block_rows, :]
        )
    query_side = convolved[0]
    key_side = convolved[1]
    value_side = convolved[2]
    product = (key_side * value_side).astype(jnp.bfloat16)
    seq_total = block_rows * lax.axis_size("ctx")
    scale_factor = 1.0 / math.sqrt(seq_total)
    arrived = regroup_out(jnp.stack([product, filters]).swapaxes(1, 2))
    per_stream = arrived.shape[1]
    grid_rows = arrived.shape[2]
    first_re, first_im = forward_transform(merged(arrived))
    prod_re = first_re[:per_stream]
    prod_im = first_im[:per_stream]
    filt_re = first_re[per_stream:]
    filt_im = first_im[per_stream:]
    mixed_re = prod_re * filt_re - prod_im * filt_im
    mixed_im = prod_re * filt_im + prod_im * filt_re
    mixed_cols = inverse_transform(mixed_re, mixed_im, grid_rows).astype(jnp.bfloat16)
    mixed_back = regroup_back(mixed_cols.reshape(1, per_stream, grid_rows, mixed_cols.shape[2]))
    mixed = mixed_back[0].T.astype(jnp.float32)
    gated = (query_side * mixed).astype(jnp.bfloat16)
    upstream = cotangent.astype(jnp.float32)
    mixed_grad = (upstream * query_side).astype(jnp.bfloat16)
    query_grad = upstream * mixed
    grad_cols = regroup_out(mixed_grad.T[None])
    grad_re, grad_im = forward_transform(merged(grad_cols))
    through_re = filt_re * grad_re + filt_im * grad_im
    through_im = filt_re * grad_im - filt_im * grad_re
    lagged_re = prod_re * grad_re + prod_im * grad_im
    lagged_im = prod_re * grad_im - prod_im * grad_re
    both_times = inverse_transform(
        jnp.concatenate([through_re, lagged_re], axis=0),
        jnp.concatenate([through_im, lagged_im], axis=0),
        grid_rows,
    )
    product_grad_cols = both_times[:per_stream].astype(jnp.bfloat16)
    filter_grad_cols = (both_times[per_stream:] * scale_factor).astype(jnp.bfloat16)
    returned = regroup_back(jnp.stack([product_grad_cols, filter_grad_cols]))
    product_grad = returned[0].T.astype(jnp.float32)
    filter_grad = returned[1].T
    conv_grad = jnp.stack([query_grad, product_grad * value_side, product_grad * key_side])
    following = shifted(conv_grad[:, :tap_reach, :].astype(jnp.bfloat16), "ctx", -1).astype(
        jnp.float32
    )
    extended_grad = jnp.concatenate([conv_grad, following], axis=1)
    running = jnp.zeros((3, block_rows, streams.shape[2]), jnp.float32)
    for offset in range(tap_reach + 1):
        running = (
            running + taps[:, offset, None, :] * extended_grad[:, offset : offset + block_rows, :]
        )
    stream_grad = running.astype(jnp.bfloat16)
    tap_terms = jnp.stack(
        [
            jnp.sum(
                conv_grad * extended[:, tap_reach - offset : tap_reach - offset + block_rows, :],
                axis=1,
            )
            for offset in range(tap_reach + 1)
        ],
        axis=1,
    )
    tap_grad = lax.psum(tap_terms, "ctx") * scale_factor
    return (gated, stream_grad, filter_grad, tap_grad)


def local(streams, taps, filters, cotangent):
    count = lax.axis_size("ctx")
    rows, channels = filters.shape
    tap_count = taps.shape[1]
    pairs_fill_lanes = channels == count * HALF and count % 2 == 0
    short_enough = rows % LANES == 0 and 8 * (rows * count) ** 2 <= TABLE_BYTES and tap_count < EDGE
    if pairs_fill_lanes and short_enough:
        return local_dense(streams, taps, filters, cotangent)
    return local_factored(streams, taps, filters, cotangent)


def solution(mesh):
    in_specs = (P(None, "ctx", "fft"), P(None, None, "fft"), P("ctx", "fft"), P("ctx", "fft"))
    out_specs = (P("ctx", "fft"), P(None, "ctx", "fft"), P("ctx", "fft"), P(None, None, "fft"))
    return jax.shard_map(local, mesh=mesh, in_specs=in_specs, out_specs=out_specs, check_vma=False)
```

```python
import functools
import math

import jax
import jax.numpy as jnp
import numpy as np
from jax import lax
from jax.experimental import pallas as pl
from jax.experimental.pallas import tpu as pltpu
from jax.sharding import PartitionSpec as P

exact_mode = lax.Precision.HIGHEST
LANES = 128
HALF = LANES // 2
EDGE = 8
TAP_ROWS = 32
TABLE_BYTES = 16 * 1024 * 1024
VMEM_BYTES = 48 * 1024 * 1024


def odd_tables(total):
    freq = 2 * np.arange(total)[:, None] + 1
    angles = (freq * np.arange(total)[None, :] % (4 * total)) * (math.pi / (2 * total))
    table = np.concatenate([np.cos(angles), -np.sin(angles)])
    high = table.astype(jnp.bfloat16)
    back = np.ascontiguousarray(table.T / total).astype(jnp.bfloat16)
    return high, back


def step_offsets(count):
    groups = count // 2
    far = groups // 2
    near = [g for g in range(1, groups) if g != far]
    order = [(far, 0)] + [(g, 1) for g in near] + [(far, 1)] + [(g, 0) for g in near] + [(0, 1)]
    return [(0, 0)] + [offset for offset in order if offset != (0, 0)]


def partner(index, offset, sign, count):
    group, member = offset
    groups = count // 2
    moved = (index // 2 + sign * group + groups) % groups
    flipped = (index + member) % 2
    return moved * 2 + flipped


def lower_lanes(rows):
    return lax.broadcasted_iota(jnp.int32, (rows, LANES), 1) < HALF


def turned(value):
    return pltpu.roll(value, HALF, 1)


def wide(value):
    return value.astype(jnp.float32)


def paired(first, second, odd, low):
    left = jnp.where(odd, turned(first), first)
    right = jnp.where(odd, second, turned(second))
    return jnp.where(low, left, right).astype(jnp.bfloat16)


def pack_kernel(count, *refs):
    in_hbm, out_refs = refs[:4], refs[4 : 5 + count]
    held, sems = refs[5 + count : 9 + count], refs[9 + count]
    copies = [pltpu.make_async_copy(here, there, sems.at[k]) for k, (here, there) in enumerate(zip(in_hbm, held))]
    for copy in copies:
        copy.start()
    for copy in copies:
        copy.wait()
    streams_ref, filters_ref, cotangent_ref, taps_ref = held
    me = lax.axis_index("ctx")
    offsets = step_offsets(count)
    rows = filters_ref.shape[0]
    half_rows = rows // 2
    tap_count = taps_ref.shape[1]
    low = lower_lanes(rows)
    low_half = lower_lanes(half_rows)
    for step in range(count):
        owner = partner(me, offsets[step], 1, count)
        cols = pl.ds(pl.multiple_of(owner // 2 * LANES, LANES), LANES)
        odd = lax.rem(owner, 2) == 1
        out = out_refs[step]
        out[0:rows, :] = paired(wide(streams_ref[1, :, cols]), wide(streams_ref[2, :, cols]), odd, low)
        out[rows : 2 * rows, :] = paired(wide(streams_ref[0, :, cols]), wide(cotangent_ref[:, cols]), odd, low)
        lag_block = wide(filters_ref[:, cols])
        out[2 * rows :, :] = paired(lag_block[:half_rows], lag_block[half_rows:], odd, low_half)
    cols = pl.ds(pl.multiple_of(me // 2 * LANES, LANES), LANES)
    odd = lax.rem(me, 2) == 1
    tap_out = out_refs[count]
    low_taps = lower_lanes(tap_count)
    here = [jnp.where(odd, turned(taps_ref[i, :, cols]), taps_ref[i, :, cols]) for i in range(3)]
    first_tap = lax.broadcasted_iota(jnp.int32, (tap_count, LANES), 0) == 0
    tap_out[...] = jnp.zeros_like(tap_out)
    tap_out[0:tap_count, :] = jnp.where(low_taps, here[1], turned(here[2]))
    tap_out[EDGE : EDGE + tap_count, :] = jnp.where(low_taps, here[0], jnp.where(first_tap, 1.0, 0.0))


def main_kernel(count, tap_count, scale, *refs):
    in_refs = refs[:count]
    tap_ref, table_hbm, back_hbm = refs[count : count + 3]
    out_refs = refs[count + 3 : 2 * count + 3]
    (raw_kv, raw_qc, conv_kv, conv_qc, signals, spectra, grad_kv, grad_q, lag_grad,
     table, back, sems) = refs[2 * count + 3 :]
    me = lax.axis_index("ctx")
    offsets = step_offsets(count)
    total = signals.shape[0]
    rows = total // count
    half_rows = rows // 2
    low = lower_lanes(rows)
    low_half = lower_lanes(half_rows)
    table_copy = pltpu.make_async_copy(table_hbm, table, sems.at[0])
    back_copy = pltpu.make_async_copy(back_hbm, back, sems.at[1])
    table_copy.start()
    back_copy.start()

    raw_kv[0:EDGE, :] = jnp.zeros((EDGE, LANES), jnp.float32)
    raw_qc[0:EDGE, :] = jnp.zeros((EDGE, LANES), jnp.float32)
    grad_kv[total:, :] = jnp.zeros((EDGE, LANES), jnp.float32)
    grad_q[total:, :] = jnp.zeros((EDGE, LANES), jnp.float32)
    for step in range(count):
        source = partner(me, offsets[step], -1, count)
        base = pl.multiple_of(source * rows, rows)
        block = in_refs[step]
        raw_kv[pl.ds(base + EDGE, rows), :] = wide(block[0:rows, :])
        raw_qc[pl.ds(base + EDGE, rows), :] = wide(block[rows : 2 * rows, :])
        lag_block = wide(block[2 * rows :, :])
        other = turned(lag_block)
        signals[pl.ds(base, half_rows), LANES:] = jnp.where(low_half, lag_block, other).astype(jnp.bfloat16)
        signals[pl.ds(base + half_rows, half_rows), LANES:] = jnp.where(low_half, other, lag_block).astype(jnp.bfloat16)

    tap_kv = [tap_ref[j : j + 1, :] for j in range(tap_count)]
    tap_q = [tap_ref[EDGE + j : EDGE + j + 1, :] for j in range(tap_count)]

    for block in range(count):
        base = block * rows
        key_value = jnp.zeros((rows, LANES), jnp.float32)
        query_cot = jnp.zeros((rows, LANES), jnp.float32)
        for j in range(tap_count):
            window = slice(base + EDGE - j, base + EDGE - j + rows)
            key_value = key_value + tap_kv[j] * raw_kv[window, :]
            query_cot = query_cot + tap_q[j] * raw_qc[window, :]
        conv_kv[base : base + rows, :] = key_value
        conv_qc[base : base + rows, :] = query_cot
        product = key_value * turned(key_value)
        mixed_grad = query_cot * turned(query_cot)
        signals[base : base + rows, :LANES] = jnp.where(low, product, mixed_grad).astype(jnp.bfloat16)

    table_copy.wait()
    part = min(256, total)
    low_part = lower_lanes(part)
    for start in range(0, total, part):
        real = jnp.dot(table[start : start + part, :], signals[...], preferred_element_type=jnp.float32)
        imag = jnp.dot(
            table[total + start : total + start + part, :], signals[...], preferred_element_type=jnp.float32
        )
        a_re, b_re = real[:, :LANES], real[:, LANES:]
        a_im, b_im = imag[:, :LANES], imag[:, LANES:]
        b_im = jnp.where(low_part, b_im, -b_im)
        r_re, r_im = turned(a_re), turned(a_im)
        spectra[start : start + part, :LANES] = (a_re * b_re - a_im * b_im).astype(jnp.bfloat16)
        spectra[start : start + part, LANES:] = (a_re * r_re + a_im * r_im).astype(jnp.bfloat16)
        spectra[total + start : total + start + part, :LANES] = (a_re * b_im + a_im * b_re).astype(jnp.bfloat16)
        spectra[total + start : total + start + part, LANES:] = (a_re * r_im - a_im * r_re).astype(jnp.bfloat16)

    back_copy.wait()
    for block in range(count):
        base = block * rows
        here = slice(base, base + rows)
        result = jnp.dot(back[here, :], spectra[...], preferred_element_type=jnp.float32)
        pair = wide(result[:, :LANES].astype(jnp.bfloat16))
        other = turned(pair)
        gated_grad = conv_qc[here, :] * jnp.where(low, pair, other)
        grad_q[here, :] = turned(gated_grad)
        grad_kv[here, :] = jnp.where(low, other, pair) * turned(conv_kv[here, :])
        lag_terms = result[:, LANES:] * scale
        lag_grad[block * half_rows : (block + 1) * half_rows, :] = jnp.where(
            low_half, lag_terms[:half_rows], turned(lag_terms[half_rows:])
        )

    tap_sum_kv = [jnp.zeros((EDGE, LANES), jnp.float32)] * tap_count
    tap_sum_q = [jnp.zeros((EDGE, LANES), jnp.float32)] * tap_count
    for step in range(count):
        owner = partner(me, offsets[step], 1, count)
        base = pl.multiple_of(owner * rows, rows)
        out = out_refs[step]
        stream_kv = jnp.zeros((rows, LANES), jnp.float32)
        stream_q = jnp.zeros((rows, LANES), jnp.float32)
        for j in range(tap_count):
            stream_kv = stream_kv + tap_kv[j] * grad_kv[pl.ds(base + j, rows), :]
            stream_q = stream_q + tap_q[j] * grad_q[pl.ds(base + j, rows), :]
        out[0:rows, :] = stream_kv.astype(jnp.bfloat16)
        out[rows : 2 * rows, :] = stream_q.astype(jnp.bfloat16)
        lag_base = pl.multiple_of(owner * half_rows, half_rows)
        out[2 * rows : 2 * rows + half_rows, :] = lag_grad[pl.ds(lag_base, half_rows), :].astype(jnp.bfloat16)
    for block in range(count):
        base = block * rows
        kv = grad_kv[base : base + rows, :]
        q = grad_q[base : base + rows, :]
        for j in range(tap_count):
            window = slice(base + EDGE - j, base + EDGE - j + rows)
            tap_sum_kv[j] = tap_sum_kv[j] + jnp.sum((kv * raw_kv[window, :]).reshape(rows // EDGE, EDGE, LANES), axis=0)
            tap_sum_q[j] = tap_sum_q[j] + jnp.sum((q * raw_qc[window, :]).reshape(rows // EDGE, EDGE, LANES), axis=0)
    spare = [jnp.zeros((1, LANES), jnp.float32)] * (EDGE - tap_count)
    sums = jnp.concatenate(
        [jnp.sum(s, axis=0, keepdims=True) for s in tap_sum_kv] + spare
        + [jnp.sum(s, axis=0, keepdims=True) for s in tap_sum_q] + spare, axis=0
    ) * scale
    high = sums.astype(jnp.bfloat16)
    both = jnp.concatenate([wide(high), sums - wide(high)], axis=0).astype(jnp.bfloat16)
    for step in range(count):
        out_refs[step][2 * rows + half_rows :, :] = both


def unpack_kernel(count, tap_count, *refs):
    in_refs = refs[:count]
    gated_ref, stream_ref, lag_ref, tap_ref = refs[count : count + 4]
    blocks = refs[count + 4]
    me = lax.axis_index("ctx")
    offsets = step_offsets(count)
    rows = gated_ref.shape[0]
    half_rows = rows // 2
    low = lower_lanes(rows)
    low_half = lower_lanes(half_rows)
    low_taps = lower_lanes(EDGE)
    for step in range(count):
        owner = partner(me, offsets[step], -1, count)
        blocks[owner, :, :] = in_refs[step][...]
    for pair in range(count // 2):
        cols = slice(pair * LANES, (pair + 1) * LANES)
        even, odd = wide(blocks[2 * pair, :, :]), wide(blocks[2 * pair + 1, :, :])
        turned_even, turned_odd = turned(even), turned(odd)

        def lower_of(window, mask):
            return jnp.where(mask, even[window], turned_odd[window])

        def upper_of(window, mask):
            return jnp.where(mask, turned_even[window], odd[window])

        key_value, query_gated = slice(0, rows), slice(rows, 2 * rows)
        stream_ref[1, :, cols] = lower_of(key_value, low).astype(jnp.bfloat16)
        stream_ref[2, :, cols] = upper_of(key_value, low).astype(jnp.bfloat16)
        stream_ref[0, :, cols] = lower_of(query_gated, low).astype(jnp.bfloat16)
        gated_ref[:, cols] = upper_of(query_gated, low).astype(jnp.bfloat16)
        lags = slice(2 * rows, 2 * rows + half_rows)
        lag_ref[0:half_rows, cols] = lower_of(lags, low_half).astype(jnp.bfloat16)
        lag_ref[half_rows:, cols] = upper_of(lags, low_half).astype(jnp.bfloat16)
        start = 2 * rows + half_rows
        high_kv, high_q, rest_kv, rest_q = [slice(start + g * EDGE, start + (g + 1) * EDGE) for g in range(4)]
        tap_ref[1, :, cols] = (lower_of(high_kv, low_taps) + lower_of(rest_kv, low_taps))[:tap_count]
        tap_ref[2, :, cols] = (upper_of(high_kv, low_taps) + upper_of(rest_kv, low_taps))[:tap_count]
        tap_ref[0, :, cols] = (lower_of(high_q, low_taps) + lower_of(rest_q, low_taps))[:tap_count]


def exchanged(blocks):
    count = len(blocks)
    return [blocks[0]] + [
        lax.ppermute(block, "ctx", [(source, partner(source, offset, 1, count)) for source in range(count)])
        for block, offset in zip(blocks[1:], step_offsets(count)[1:])
    ]


def in_hbm(array):
    return pltpu.with_memory_space_constraint(array, pltpu.HBM)


def in_vmem(count):
    return [pl.BlockSpec(memory_space=pltpu.VMEM)] * count


def local_dense(streams, taps, filters, cotangent):
    count = lax.axis_size("ctx")
    rows, channels = filters.shape
    tap_count = taps.shape[1]
    total = rows * count
    params = pltpu.CompilerParams(vmem_limit_bytes=VMEM_BYTES)
    sent_rows = 2 * rows + rows // 2
    packed = pl.pallas_call(
        functools.partial(pack_kernel, count),
        out_shape=[jax.ShapeDtypeStruct((sent_rows, LANES), jnp.bfloat16)] * count
        + [jax.ShapeDtypeStruct((2 * EDGE, LANES), jnp.float32)],
        in_specs=[pl.BlockSpec(memory_space=pltpu.HBM)] * 4,
        out_specs=in_vmem(count + 1),
        scratch_shapes=[pltpu.VMEM(a.shape, a.dtype) for a in (streams, filters, cotangent, taps)]
        + [pltpu.SemaphoreType.DMA((4,))],
        compiler_params=params,
        name="pack",
    )(*[in_hbm(a) for a in (streams, filters, cotangent, taps)])
    arrived = exchanged(packed[:count])
    table, back = odd_tables(total)
    back_rows = sent_rows + TAP_ROWS
    f32_rows = lambda extent: pltpu.VMEM((extent, LANES), jnp.float32)
    made = pl.pallas_call(
        functools.partial(main_kernel, count, tap_count, 1.0 / math.sqrt(total)),
        out_shape=[jax.ShapeDtypeStruct((back_rows, LANES), jnp.bfloat16)] * count,
        in_specs=in_vmem(count + 1) + [pl.BlockSpec(memory_space=pltpu.HBM)] * 2,
        out_specs=in_vmem(count),
        scratch_shapes=[
            f32_rows(total + EDGE), f32_rows(total + EDGE), f32_rows(total), f32_rows(total),
            pltpu.VMEM((total, 2 * LANES), jnp.bfloat16), pltpu.VMEM((2 * total, 2 * LANES), jnp.bfloat16),
            f32_rows(total + EDGE), f32_rows(total + EDGE), f32_rows(total // 2),
            pltpu.VMEM(table.shape, jnp.bfloat16), pltpu.VMEM(back.shape, jnp.bfloat16),
            pltpu.SemaphoreType.DMA((2,)),
        ],
        compiler_params=params,
        name="channels",
    )(*arrived, packed[count], in_hbm(jnp.asarray(table)), in_hbm(jnp.asarray(back)))
    returned = exchanged(made)
    return tuple(
        pl.pallas_call(
            functools.partial(unpack_kernel, count, tap_count),
            out_shape=[
                jax.ShapeDtypeStruct(filters.shape, jnp.bfloat16),
                jax.ShapeDtypeStruct(streams.shape, jnp.bfloat16),
                jax.ShapeDtypeStruct(filters.shape, jnp.bfloat16),
                jax.ShapeDtypeStruct(taps.shape, jnp.float32),
            ],
            in_specs=in_vmem(count),
            out_specs=in_vmem(4),
            scratch_shapes=[pltpu.VMEM((count, back_rows, LANES), jnp.bfloat16)],
            compiler_params=params,
            name="unpack",
        )(*returned)
    )


def shifted(value, axis, steps):
    count = lax.axis_size(axis)
    first, last = (max(0, -steps), min(count, count - steps))
    return lax.ppermute(value, axis, [(source, source + steps) for source in range(first, last)])


def angle_table(row_count, col_count, col_start, period):
    row_ids = lax.iota(jnp.int32, row_count)
    col_ids = col_start + lax.iota(jnp.int32, col_count)
    turns = row_ids[:, None] * col_ids[None, :] % period
    angles = turns.astype(jnp.float32) * (2.0 * math.pi / period)
    return (jnp.cos(angles), jnp.sin(angles))


def column_start():
    return 0


def split_product(table, signal):
    high_part = table.astype(jnp.bfloat16)
    low_part = (table - high_part.astype(jnp.float32)).astype(jnp.bfloat16)
    first = jnp.einsum("kt,ctu->cku", high_part, signal, preferred_element_type=jnp.float32)
    second = jnp.einsum("kt,ctu->cku", low_part, signal, preferred_element_type=jnp.float32)
    return first + second


def forward_transform(signal):
    input_rows = signal.shape[1]
    row_count = 2 * input_rows
    col_count = signal.shape[2]
    period = row_count * col_count
    cos_first, sin_first = angle_table(row_count, input_rows, 0, row_count)
    first_re = split_product(cos_first, signal)
    first_im = -split_product(sin_first, signal)
    cos_twist, sin_twist = angle_table(row_count, col_count, column_start(), period)
    turned_re = first_re * cos_twist + first_im * sin_twist
    turned_im = first_im * cos_twist - first_re * sin_twist
    cos_second, sin_second = angle_table(col_count, col_count, 0, col_count)
    spec_re = jnp.einsum("cut,tk->cuk", turned_re, cos_second, precision=exact_mode) + jnp.einsum(
        "cut,tk->cuk", turned_im, sin_second, precision=exact_mode
    )
    spec_im = jnp.einsum("cut,tk->cuk", turned_im, cos_second, precision=exact_mode) - jnp.einsum(
        "cut,tk->cuk", turned_re, sin_second, precision=exact_mode
    )
    return (spec_re, spec_im)


def inverse_transform(spec_re, spec_im, keep_rows):
    full_width = spec_re.shape[2]
    cos_second, sin_second = angle_table(full_width, full_width, 0, full_width)
    back_re = jnp.einsum("cuk,kt->cut", spec_re, cos_second, precision=exact_mode) - jnp.einsum(
        "cuk,kt->cut", spec_im, sin_second, precision=exact_mode
    )
    back_im = jnp.einsum("cuk,kt->cut", spec_im, cos_second, precision=exact_mode) + jnp.einsum(
        "cuk,kt->cut", spec_re, sin_second, precision=exact_mode
    )
    row_count = back_re.shape[1]
    col_count = back_re.shape[2]
    period = row_count * full_width
    cos_twist, sin_twist = angle_table(row_count, col_count, column_start(), period)
    turned_re = back_re * cos_twist - back_im * sin_twist
    turned_im = back_im * cos_twist + back_re * sin_twist
    cos_first, sin_first = angle_table(keep_rows, row_count, 0, row_count)
    result = jnp.einsum("tk,cku->ctu", cos_first, turned_re, precision=exact_mode) - jnp.einsum(
        "tk,cku->ctu", sin_first, turned_im, precision=exact_mode
    )
    return result * (1.0 / period)


def regroup_out(stacked):
    count_here = stacked.shape[0]
    channel_count = stacked.shape[1]
    block_rows = stacked.shape[2]
    shaped = stacked.reshape(count_here, channel_count, 1, block_rows)
    return lax.all_to_all(shaped, "ctx", split_axis=1, concat_axis=2, tiled=True)


def regroup_back(stacked):
    count_here = stacked.shape[0]
    arrived = lax.all_to_all(stacked, "ctx", split_axis=2, concat_axis=1, tiled=True)
    return arrived.reshape(count_here, arrived.shape[1], arrived.shape[3])


def merged(block):
    return block.reshape(block.shape[0] * block.shape[1], block.shape[2], block.shape[3])


def local_factored(streams, taps, filters, cotangent):
    block_rows = streams.shape[1]
    tap_reach = taps.shape[1] - 1
    earlier = shifted(streams[:, block_rows - tap_reach :, :], "ctx", 1)
    extended = jnp.concatenate([earlier, streams], axis=1).astype(jnp.float32)
    convolved = jnp.zeros((3, block_rows, streams.shape[2]), jnp.float32)
    for offset in range(tap_reach + 1):
        convolved = (
            convolved
            + taps[:, offset, None, :]
            * extended[:, tap_reach - offset : tap_reach - offset + block_rows, :]
        )
    query_side = convolved[0]
    key_side = convolved[1]
    value_side = convolved[2]
    product = (key_side * value_side).astype(jnp.bfloat16)
    seq_total = block_rows * lax.axis_size("ctx")
    scale_factor = 1.0 / math.sqrt(seq_total)
    arrived = regroup_out(jnp.stack([product, filters]).swapaxes(1, 2))
    per_stream = arrived.shape[1]
    grid_rows = arrived.shape[2]
    first_re, first_im = forward_transform(merged(arrived))
    prod_re = first_re[:per_stream]
    prod_im = first_im[:per_stream]
    filt_re = first_re[per_stream:]
    filt_im = first_im[per_stream:]
    mixed_re = prod_re * filt_re - prod_im * filt_im
    mixed_im = prod_re * filt_im + prod_im * filt_re
    mixed_cols = inverse_transform(mixed_re, mixed_im, grid_rows).astype(jnp.bfloat16)
    mixed_back = regroup_back(mixed_cols.reshape(1, per_stream, grid_rows, mixed_cols.shape[2]))
    mixed = mixed_back[0].T.astype(jnp.float32)
    gated = (query_side * mixed).astype(jnp.bfloat16)
    upstream = cotangent.astype(jnp.float32)
    mixed_grad = (upstream * query_side).astype(jnp.bfloat16)
    query_grad = upstream * mixed
    grad_cols = regroup_out(mixed_grad.T[None])
    grad_re, grad_im = forward_transform(merged(grad_cols))
    through_re = filt_re * grad_re + filt_im * grad_im
    through_im = filt_re * grad_im - filt_im * grad_re
    lagged_re = prod_re * grad_re + prod_im * grad_im
    lagged_im = prod_re * grad_im - prod_im * grad_re
    both_times = inverse_transform(
        jnp.concatenate([through_re, lagged_re], axis=0),
        jnp.concatenate([through_im, lagged_im], axis=0),
        grid_rows,
    )
    product_grad_cols = both_times[:per_stream].astype(jnp.bfloat16)
    filter_grad_cols = (both_times[per_stream:] * scale_factor).astype(jnp.bfloat16)
    returned = regroup_back(jnp.stack([product_grad_cols, filter_grad_cols]))
    product_grad = returned[0].T.astype(jnp.float32)
    filter_grad = returned[1].T
    conv_grad = jnp.stack([query_grad, product_grad * value_side, product_grad * key_side])
    following = shifted(conv_grad[:, :tap_reach, :].astype(jnp.bfloat16), "ctx", -1).astype(
        jnp.float32
    )
    extended_grad = jnp.concatenate([conv_grad, following], axis=1)
    running = jnp.zeros((3, block_rows, streams.shape[2]), jnp.float32)
    for offset in range(tap_reach + 1):
        running = (
            running + taps[:, offset, None, :] * extended_grad[:, offset : offset + block_rows, :]
        )
    stream_grad = running.astype(jnp.bfloat16)
    tap_terms = jnp.stack(
        [
            jnp.sum(
                conv_grad * extended[:, tap_reach - offset : tap_reach - offset + block_rows, :],
                axis=1,
            )
            for offset in range(tap_reach + 1)
        ],
        axis=1,
    )
    tap_grad = lax.psum(tap_terms, "ctx") * scale_factor
    return (gated, stream_grad, filter_grad, tap_grad)


def local(streams, taps, filters, cotangent):
    count = lax.axis_size("ctx")
    rows, channels = filters.shape
    tap_count = taps.shape[1]
    pairs_fill_lanes = channels == count * HALF and count % 2 == 0
    short_enough = rows % LANES == 0 and 8 * (rows * count) ** 2 <= TABLE_BYTES and tap_count < EDGE
    if pairs_fill_lanes and short_enough:
        return local_dense(streams, taps, filters, cotangent)
    return local_factored(streams, taps, filters, cotangent)


def solution(mesh):
    in_specs = (P(None, "ctx", "fft"), P(None, None, "fft"), P("ctx", "fft"), P("ctx", "fft"))
    out_specs = (P("ctx", "fft"), P(None, "ctx", "fft"), P("ctx", "fft"), P(None, None, "fft"))
    return jax.shard_map(local, mesh=mesh, in_specs=in_specs, out_specs=out_specs, check_vma=False)
```

```python
import functools
import math

import jax
import jax.numpy as jnp
import numpy as np
from jax import lax
from jax.experimental import pallas as pl
from jax.experimental.pallas import tpu as pltpu
from jax.sharding import PartitionSpec as P

exact_mode = lax.Precision.HIGHEST
LANES = 128
HALF = LANES // 2
PHASES = 4
EDGE = 8
TABLE_BYTES = 16 * 1024 * 1024
VMEM_BYTES = 32 * 1024 * 1024


def step_offsets(count):
    groups = count // 2
    far = groups // 2
    near = [g for g in range(1, groups) if g != far]
    order = [(g, 0) for g in near[:1]] + [(far, 0), (far, 1)] + [(g, 1) for g in near]
    order = order + [(0, 1)] + [(g, 0) for g in near[1:]]
    return [(0, 0)] + [offset for offset in order if offset != (0, 0)]


def partner(index, offset, sign, count):
    group, member = offset
    groups = count // 2
    moved = (index // 2 + sign * group + groups) % groups
    flipped = (index + member) % 2
    return moved * 2 + flipped


def lower_lanes(rows):
    return lax.broadcasted_iota(jnp.int32, (rows, LANES), 1) < HALF


def turned(value):
    return pltpu.roll(value, HALF, 1)


def wide(value):
    return value.astype(jnp.float32)


def paired(first, second, odd, low):
    left = jnp.where(odd, turned(first), first)
    right = jnp.where(odd, second, turned(second))
    return jnp.where(low, left, right).astype(jnp.bfloat16)


def pack_kernel(count, *refs):
    in_hbm, out_refs = refs[:4], refs[4 : 5 + count]
    held, sems = refs[5 + count : 9 + count], refs[9 + count]
    copies = [pltpu.make_async_copy(here, there, sems.at[k]) for k, (here, there) in enumerate(zip(in_hbm, held))]
    for copy in copies:
        copy.start()
    for copy in copies:
        copy.wait()
    streams_ref, filters_ref, cotangent_ref, taps_ref = held
    me = lax.axis_index("ctx")
    offsets = step_offsets(count)
    rows = filters_ref.shape[0]
    half_rows = rows // 2
    tap_count = taps_ref.shape[1]
    low = lower_lanes(rows)
    low_half = lower_lanes(half_rows)
    for step in range(count):
        owner = partner(me, offsets[step], 1, count)
        cols = pl.ds(pl.multiple_of(owner // 2 * LANES, LANES), LANES)
        odd = lax.rem(owner, 2) == 1
        out = out_refs[step]
        out[0:rows, :] = paired(wide(streams_ref[1, :, cols]), wide(streams_ref[2, :, cols]), odd, low)
        out[rows : 2 * rows, :] = paired(wide(streams_ref[0, :, cols]), wide(cotangent_ref[:, cols]), odd, low)
        lag_block = wide(filters_ref[:, cols])
        out[2 * rows :, :] = paired(lag_block[:half_rows], lag_block[half_rows:], odd, low_half)
    cols = pl.ds(pl.multiple_of(me // 2 * LANES, LANES), LANES)
    odd = lax.rem(me, 2) == 1
    tap_out = out_refs[count]
    low_taps = lower_lanes(tap_count)
    here = [jnp.where(odd, turned(taps_ref[i, :, cols]), taps_ref[i, :, cols]) for i in range(3)]
    first_tap = lax.broadcasted_iota(jnp.int32, (tap_count, LANES), 0) == 0
    tap_out[...] = jnp.zeros_like(tap_out)
    tap_out[0:tap_count, :] = jnp.where(low_taps, here[1], turned(here[2]))
    tap_out[EDGE : EDGE + tap_count, :] = jnp.where(low_taps, here[0], jnp.where(first_tap, 1.0, 0.0))


def phase_tables(total):
    quarter = total // PHASES
    freq = 2 * np.arange(quarter)[:, None] + 1
    ahead, back = [], []
    for phase in range(PHASES):
        place = PHASES * np.arange(quarter)[None, :] + phase
        angles = (freq * place % (4 * total)) * (math.pi / (2 * total))
        table = np.concatenate([np.cos(angles), -np.sin(angles)])
        ahead.append(table)
        back.append(table.T / total)
    ahead = np.stack(ahead)
    high = ahead.astype(jnp.bfloat16)
    rest = (ahead - high.astype(np.float64)).astype(jnp.bfloat16)
    return high, rest, np.stack(back).astype(jnp.bfloat16)


def quarter_turns(parts):
    (r0, i0), (r1, i1), (r2, i2), (r3, i3) = parts
    even_r, even_i, odd_r, odd_i = r0 + r2, i0 + i2, r1 + r3, i1 + i3
    gap_r, gap_i, side_r, side_i = r0 - r2, i0 - i2, r1 - r3, i1 - i3
    return [
        (even_r + odd_r, even_i + odd_i),
        (gap_r - side_i, gap_i + side_r),
        (even_r - odd_r, even_i - odd_i),
        (gap_r + side_i, gap_i - side_r),
    ]


def main_kernel(count, tap_count, scale, *refs):
    in_refs = refs[:count]
    tap_ref, high, rest, back = refs[count : count + 4]
    out_refs = refs[count + 4 : 2 * count + 4]
    (raw_kv, raw_qc, raw_lag, conv_kv, conv_qc, signals, phased, spectra, pairs, grad_kv, grad_q, lag_grad) = refs[
        2 * count + 4 :
    ]
    me = lax.axis_index("ctx")
    offsets = step_offsets(count)
    total = raw_lag.shape[0]
    quarter = total // PHASES
    rows = total // count
    half_rows = rows // 2
    low_half = lower_lanes(half_rows)

    raw_kv[0:EDGE, :] = jnp.zeros((EDGE, LANES), jnp.float32)
    raw_qc[0:EDGE, :] = jnp.zeros((EDGE, LANES), jnp.float32)
    grad_kv[total:, :] = jnp.zeros((EDGE, LANES), jnp.float32)
    grad_q[total:, :] = jnp.zeros((EDGE, LANES), jnp.float32)
    for step in range(count):
        source = partner(me, offsets[step], -1, count)
        base = pl.multiple_of(source * rows, rows)
        block = in_refs[step]
        raw_kv[pl.ds(base + EDGE, rows), :] = wide(block[0:rows, :])
        raw_qc[pl.ds(base + EDGE, rows), :] = wide(block[rows : 2 * rows, :])
        lag_block = wide(block[2 * rows :, :])
        other = turned(lag_block)
        raw_lag[pl.ds(base, half_rows), :] = jnp.where(low_half, lag_block, other)
        raw_lag[pl.ds(base + half_rows, half_rows), :] = jnp.where(low_half, other, lag_block)

    tap_kv = [tap_ref[j : j + 1, :] for j in range(tap_count)]
    tap_q = [tap_ref[EDGE + j : EDGE + j + 1, :] for j in range(tap_count)]

    part = min(32, quarter)
    low = lower_lanes(part)
    for start in range(0, quarter, part):
        for phase in range(PHASES):
            first = PHASES * start + phase
            here = slice(phase * quarter + start, phase * quarter + start + part)
            key_value = jnp.zeros((part, LANES), jnp.float32)
            query_cot = jnp.zeros((part, LANES), jnp.float32)
            for j in range(tap_count):
                window = pl.ds(first + EDGE - j, part, stride=PHASES)
                key_value = key_value + tap_kv[j] * raw_kv[window, :]
                query_cot = query_cot + tap_q[j] * raw_qc[window, :]
            conv_kv[here, :] = key_value
            conv_qc[here, :] = query_cot
            product = key_value * turned(key_value)
            mixed_grad = query_cot * turned(query_cot)
            signals[here, :LANES] = jnp.where(low, product, mixed_grad).astype(jnp.bfloat16)
            signals[here, LANES:] = raw_lag[pl.ds(first, part, stride=PHASES), :].astype(jnp.bfloat16)

    for phase in range(PHASES):
        signal = signals[phase * quarter : (phase + 1) * quarter, :]
        phased[phase, :, :] = jnp.dot(high[phase], signal, preferred_element_type=jnp.float32) + jnp.dot(
            rest[phase], signal, preferred_element_type=jnp.float32
        )

    part = min(16, quarter)
    low = lower_lanes(part)
    for start in range(0, quarter, part):
        real, imag = slice(start, start + part), slice(quarter + start, quarter + start + part)
        signal_turns = quarter_turns([(phased[p, real, :LANES], phased[p, imag, :LANES]) for p in range(PHASES)])
        lag_turns = quarter_turns([(phased[p, real, LANES:], phased[p, imag, LANES:]) for p in range(PHASES)])
        through, lagged = [], []
        for (a_re, a_im), (b_re, b_im) in zip(signal_turns, lag_turns):
            b_im = jnp.where(low, b_im, -b_im)
            r_re, r_im = turned(a_re), turned(a_im)
            through.append((a_re * b_re - a_im * b_im, a_re * b_im + a_im * b_re))
            lagged.append((a_re * r_re + a_im * r_im, a_re * r_im - a_im * r_re))
        for cols, parts in ((slice(0, LANES), through), (slice(LANES, 2 * LANES), lagged)):
            turns = quarter_turns(parts)
            for phase in range(PHASES):
                value_re, value_im = turns[-phase % PHASES]
                spectra[phase, real, cols] = value_re.astype(jnp.bfloat16)
                spectra[phase, imag, cols] = value_im.astype(jnp.bfloat16)

    low = lower_lanes(quarter)
    for phase in range(PHASES):
        here = slice(phase * quarter, (phase + 1) * quarter)
        spread = pl.ds(phase, quarter, stride=PHASES)
        result = jnp.dot(back[phase], spectra[phase], preferred_element_type=jnp.float32)
        pair = wide(result[:, :LANES].astype(jnp.bfloat16))
        other = turned(pair)
        pairs[spread, :] = pair
        grad_q[spread, :] = turned(conv_qc[here, :]) * jnp.where(low, pair, other)
        grad_kv[spread, :] = jnp.where(low, other, pair) * turned(conv_kv[here, :])
        lag_grad[spread, :] = result[:, LANES:] * scale

    tap_sum_kv = [jnp.zeros((EDGE, LANES), jnp.float32)] * tap_count
    tap_sum_q = [jnp.zeros((EDGE, LANES), jnp.float32)] * tap_count
    part = min(32, rows)
    for base in range(0, total, part):
        kv = grad_kv[base : base + part, :]
        q = grad_q[base : base + part, :]
        for j in range(tap_count):
            window = slice(base + EDGE - j, base + EDGE - j + part)
            tap_sum_kv[j] = tap_sum_kv[j] + jnp.sum((kv * raw_kv[window, :]).reshape(part // EDGE, EDGE, LANES), axis=0)
            tap_sum_q[j] = tap_sum_q[j] + jnp.sum((q * raw_qc[window, :]).reshape(part // EDGE, EDGE, LANES), axis=0)
    spare = [jnp.zeros((1, LANES), jnp.float32)] * (EDGE - tap_count)
    sums = [
        jnp.concatenate([jnp.sum(s, axis=0, keepdims=True) for s in parts] + spare, axis=0) * scale
        for parts in (tap_sum_kv, tap_sum_q)
    ]
    sums_high = [wide(s.astype(jnp.bfloat16)) for s in sums]
    low_edge = lower_lanes(EDGE)
    sums_q = jnp.where(low_edge, sums_high[1], turned(sums[1] - sums_high[1]))
    for step in range(count):
        owner = partner(me, offsets[step], 1, count)
        base = pl.multiple_of(owner * rows, rows)
        out = out_refs[step]
        out[0:rows, :] = pairs[pl.ds(base, rows), :].astype(jnp.bfloat16)
        out[rows : rows + half_rows, :] = jnp.where(
            low_half, lag_grad[pl.ds(base, half_rows), :], turned(lag_grad[pl.ds(base + half_rows, half_rows), :])
        ).astype(jnp.bfloat16)
        edge_q = jnp.where(
            low_edge, raw_qc[pl.ds(base, EDGE), :], turned(grad_q[pl.ds(base + rows, EDGE), :])
        )
        extra = [raw_kv[pl.ds(base, EDGE), :], grad_kv[pl.ds(base + rows, EDGE), :], edge_q]
        extra = extra + [sums_high[0], sums[0] - sums_high[0], sums_q]
        out[rows + half_rows :, :] = jnp.concatenate(extra, axis=0).astype(jnp.bfloat16)


def shifted_sum(taps, padded, first, direction, rows):
    return sum(taps[j] * padded[first + direction * j : first + direction * j + rows, :] for j in range(len(taps)))


def local_kernel(tap_count, streams_hbm, taps_hbm, cotangent_hbm, high_hbm, rest_hbm, back_hbm, arrived_ref, *refs):
    conv_ref, taps_ref, cotangent_ref, high_ref, rest_ref, back_ref, streams_ref, padded, sems = refs
    pairs = (
        (streams_hbm, streams_ref), (taps_hbm, taps_ref), (cotangent_hbm, cotangent_ref),
        (high_hbm, high_ref), (rest_hbm, rest_ref), (back_hbm, back_ref),
    )
    copies = [pltpu.make_async_copy(here, there, sems.at[k]) for k, (here, there) in enumerate(pairs)]
    for copy in copies:
        copy.start()
    copies[0].wait()
    copies[1].wait()
    streams, rows, channels = conv_ref.shape
    padded[0:EDGE, :] = jnp.zeros((EDGE, LANES), jnp.float32)
    for i in range(streams):
        for start in range(0, channels, LANES):
            cols = slice(start, start + LANES)
            padded[EDGE:, :] = wide(streams_ref[i, :, cols])
            taps = [taps_ref[i, j : j + 1, cols] for j in range(tap_count)]
            conv_ref[i, :, cols] = shifted_sum(taps, padded, EDGE, -1, rows)
    for copy in copies[2:]:
        copy.wait()


def finish_kernel(count, tap_count, *refs):
    in_refs = refs[:count]
    conv_ref, taps_ref, cotangent_ref = refs[count : count + 3]
    gated_ref, stream_ref, lag_ref, tap_ref = refs[count + 3 : count + 7]
    blocks, edges, grads = refs[count + 7 :]
    me = lax.axis_index("ctx")
    offsets = step_offsets(count)
    rows = gated_ref.shape[0]
    half_rows = rows // 2
    low = lower_lanes(rows)
    low_half = lower_lanes(half_rows)
    low_edge = lower_lanes(EDGE)
    for step in range(count):
        owner = partner(me, offsets[step], -1, count)
        blocks[owner, :, :] = in_refs[step][...]
    edges[EDGE:, :] = jnp.zeros((EDGE, LANES), jnp.float32)
    for pair in range(count // 2):
        cols = slice(pair * LANES, (pair + 1) * LANES)

        def both(start, extent, mask):
            window = slice(start, start + extent)
            even, odd = wide(blocks[2 * pair, window, :]), wide(blocks[2 * pair + 1, window, :])
            return jnp.where(mask, even, turned(odd)), jnp.where(mask, turned(even), odd)

        start = rows + half_rows
        mixed, product_grad = both(0, rows, low)
        lag_lower, lag_upper = both(rows, half_rows, low_half)
        lag_ref[0:half_rows, cols] = lag_lower.astype(jnp.bfloat16)
        lag_ref[half_rows:, cols] = lag_upper.astype(jnp.bfloat16)
        before_key, before_value = both(start, EDGE, low_edge)
        after_key, after_value = both(start + EDGE, EDGE, low_edge)
        before_query, after_query = both(start + 2 * EDGE, EDGE, low_edge)
        taps = [[taps_ref[i, j : j + 1, cols] for j in range(tap_count)] for i in range(3)]
        convolved = []
        for i, before in enumerate((before_query, before_key, before_value)):
            edges[0:EDGE, :] = before
            first = conv_ref[i, 0:EDGE, cols] + shifted_sum(taps[i], edges, EDGE, -1, EDGE)
            convolved.append(jnp.concatenate([first, conv_ref[i, EDGE:, cols]], axis=0))
        query, key, value = convolved
        gated_ref[:, cols] = (query * mixed).astype(jnp.bfloat16)
        own = (wide(cotangent_ref[:, cols]) * mixed, product_grad * value, product_grad * key)
        for i, after in enumerate((after_query, after_key, after_value)):
            grads[i, 0:rows, :] = own[i]
            grads[i, rows:, :] = after
            stream_ref[i, :, cols] = shifted_sum(taps[i], grads.at[i], 0, 1, rows).astype(jnp.bfloat16)
        high_key, high_value = both(start + 3 * EDGE, EDGE, low_edge)
        rest_key, rest_value = both(start + 4 * EDGE, EDGE, low_edge)
        tap_ref[1, :, cols] = (high_key + rest_key)[:tap_count]
        tap_ref[2, :, cols] = (high_value + rest_value)[:tap_count]
        query_parts = [wide(blocks[2 * pair + k, start + 5 * EDGE : start + 6 * EDGE, :]) for k in range(2)]
        query_sums = [part + turned(part) for part in query_parts]
        tap_ref[0, :, cols] = jnp.where(low_edge, query_sums[0], query_sums[1])[:tap_count]


def exchanged(blocks):
    count = len(blocks)
    return [blocks[0]] + [
        lax.ppermute(block, "ctx", [(source, partner(source, offset, 1, count)) for source in range(count)])
        for block, offset in zip(blocks[1:], step_offsets(count)[1:])
    ]


def in_hbm(array):
    return pltpu.with_memory_space_constraint(array, pltpu.HBM)


def in_vmem(count):
    return [pl.BlockSpec(memory_space=pltpu.VMEM)] * count


def local_dense(streams, taps, filters, cotangent):
    count = lax.axis_size("ctx")
    rows, channels = filters.shape
    tap_count = taps.shape[1]
    total = rows * count
    params = pltpu.CompilerParams(vmem_limit_bytes=VMEM_BYTES)
    sent_rows = 2 * rows + rows // 2
    packed = pl.pallas_call(
        functools.partial(pack_kernel, count),
        out_shape=[jax.ShapeDtypeStruct((sent_rows, LANES), jnp.bfloat16)] * count
        + [jax.ShapeDtypeStruct((2 * EDGE, LANES), jnp.float32)],
        in_specs=[pl.BlockSpec(memory_space=pltpu.HBM)] * 4,
        out_specs=in_vmem(count + 1),
        scratch_shapes=[pltpu.VMEM(a.shape, a.dtype) for a in (streams, filters, cotangent, taps)]
        + [pltpu.SemaphoreType.DMA((4,))],
        compiler_params=params,
        name="pack",
    )(*[in_hbm(a) for a in (streams, filters, cotangent, taps)])
    arrived = exchanged(packed[:count])
    quarter = total // PHASES
    tables = phase_tables(total)
    hbm = pl.BlockSpec(memory_space=pltpu.HBM)
    conv, taps_here, cotangent_here, *tables_here = pl.pallas_call(
        functools.partial(local_kernel, tap_count),
        out_shape=[
            jax.ShapeDtypeStruct(streams.shape, jnp.float32),
            jax.ShapeDtypeStruct(taps.shape, taps.dtype),
            jax.ShapeDtypeStruct(cotangent.shape, cotangent.dtype),
            *[jax.ShapeDtypeStruct(table.shape, jnp.bfloat16) for table in tables],
        ],
        in_specs=[hbm] * (3 + len(tables)) + [pl.BlockSpec(memory_space=pl.ANY)],
        out_specs=in_vmem(3 + len(tables)),
        scratch_shapes=[
            pltpu.VMEM(streams.shape, streams.dtype),
            pltpu.VMEM((rows + EDGE, LANES), jnp.float32),
            pltpu.SemaphoreType.DMA((3 + len(tables),)),
        ],
        compiler_params=params,
        name="local",
    )(*[in_hbm(jnp.asarray(a)) for a in (streams, taps, cotangent, *tables)], arrived[count - 2])
    back_rows = rows + rows // 2 + 6 * EDGE
    f32_rows = lambda extent: pltpu.VMEM((extent, LANES), jnp.float32)
    made = pl.pallas_call(
        functools.partial(main_kernel, count, tap_count, 1.0 / math.sqrt(total)),
        out_shape=[jax.ShapeDtypeStruct((back_rows, LANES), jnp.bfloat16)] * count,
        in_specs=in_vmem(count + 1 + len(tables)),
        out_specs=in_vmem(count),
        scratch_shapes=[
            f32_rows(total + EDGE), f32_rows(total + EDGE), f32_rows(total), f32_rows(total), f32_rows(total),
            pltpu.VMEM((total, 2 * LANES), jnp.bfloat16),
            pltpu.VMEM((PHASES, 2 * quarter, 2 * LANES), jnp.float32),
            pltpu.VMEM((PHASES, 2 * quarter, 2 * LANES), jnp.bfloat16),
            f32_rows(total), f32_rows(total + EDGE), f32_rows(total + EDGE), f32_rows(total),
        ],
        compiler_params=params,
        name="channels",
    )(*arrived, packed[count], *tables_here)
    returned = exchanged(made)
    return tuple(
        pl.pallas_call(
            functools.partial(finish_kernel, count, tap_count),
            out_shape=[
                jax.ShapeDtypeStruct(filters.shape, jnp.bfloat16),
                jax.ShapeDtypeStruct(streams.shape, jnp.bfloat16),
                jax.ShapeDtypeStruct(filters.shape, jnp.bfloat16),
                jax.ShapeDtypeStruct(taps.shape, jnp.float32),
            ],
            in_specs=in_vmem(count + 3),
            out_specs=in_vmem(4),
            scratch_shapes=[
                pltpu.VMEM((count, back_rows, LANES), jnp.bfloat16),
                f32_rows(2 * EDGE),
                pltpu.VMEM((3, rows + EDGE, LANES), jnp.float32),
            ],
            compiler_params=params,
            name="finish",
        )(*returned, conv, taps_here, cotangent_here)
    )


def shifted(value, axis, steps):
    count = lax.axis_size(axis)
    first, last = (max(0, -steps), min(count, count - steps))
    return lax.ppermute(value, axis, [(source, source + steps) for source in range(first, last)])


def angle_table(row_count, col_count, col_start, period):
    row_ids = lax.iota(jnp.int32, row_count)
    col_ids = col_start + lax.iota(jnp.int32, col_count)
    turns = row_ids[:, None] * col_ids[None, :] % period
    angles = turns.astype(jnp.float32) * (2.0 * math.pi / period)
    return (jnp.cos(angles), jnp.sin(angles))


def column_start():
    return 0


def split_product(table, signal):
    high_part = table.astype(jnp.bfloat16)
    low_part = (table - high_part.astype(jnp.float32)).astype(jnp.bfloat16)
    first = jnp.einsum("kt,ctu->cku", high_part, signal, preferred_element_type=jnp.float32)
    second = jnp.einsum("kt,ctu->cku", low_part, signal, preferred_element_type=jnp.float32)
    return first + second


def forward_transform(signal):
    input_rows = signal.shape[1]
    row_count = 2 * input_rows
    col_count = signal.shape[2]
    period = row_count * col_count
    cos_first, sin_first = angle_table(row_count, input_rows, 0, row_count)
    first_re = split_product(cos_first, signal)
    first_im = -split_product(sin_first, signal)
    cos_twist, sin_twist = angle_table(row_count, col_count, column_start(), period)
    turned_re = first_re * cos_twist + first_im * sin_twist
    turned_im = first_im * cos_twist - first_re * sin_twist
    cos_second, sin_second = angle_table(col_count, col_count, 0, col_count)
    spec_re = jnp.einsum("cut,tk->cuk", turned_re, cos_second, precision=exact_mode) + jnp.einsum(
        "cut,tk->cuk", turned_im, sin_second, precision=exact_mode
    )
    spec_im = jnp.einsum("cut,tk->cuk", turned_im, cos_second, precision=exact_mode) - jnp.einsum(
        "cut,tk->cuk", turned_re, sin_second, precision=exact_mode
    )
    return (spec_re, spec_im)


def inverse_transform(spec_re, spec_im, keep_rows):
    full_width = spec_re.shape[2]
    cos_second, sin_second = angle_table(full_width, full_width, 0, full_width)
    back_re = jnp.einsum("cuk,kt->cut", spec_re, cos_second, precision=exact_mode) - jnp.einsum(
        "cuk,kt->cut", spec_im, sin_second, precision=exact_mode
    )
    back_im = jnp.einsum("cuk,kt->cut", spec_im, cos_second, precision=exact_mode) + jnp.einsum(
        "cuk,kt->cut", spec_re, sin_second, precision=exact_mode
    )
    row_count = back_re.shape[1]
    col_count = back_re.shape[2]
    period = row_count * full_width
    cos_twist, sin_twist = angle_table(row_count, col_count, column_start(), period)
    turned_re = back_re * cos_twist - back_im * sin_twist
    turned_im = back_im * cos_twist + back_re * sin_twist
    cos_first, sin_first = angle_table(keep_rows, row_count, 0, row_count)
    result = jnp.einsum("tk,cku->ctu", cos_first, turned_re, precision=exact_mode) - jnp.einsum(
        "tk,cku->ctu", sin_first, turned_im, precision=exact_mode
    )
    return result * (1.0 / period)


def regroup_out(stacked):
    count_here = stacked.shape[0]
    channel_count = stacked.shape[1]
    block_rows = stacked.shape[2]
    shaped = stacked.reshape(count_here, channel_count, 1, block_rows)
    return lax.all_to_all(shaped, "ctx", split_axis=1, concat_axis=2, tiled=True)


def regroup_back(stacked):
    count_here = stacked.shape[0]
    arrived = lax.all_to_all(stacked, "ctx", split_axis=2, concat_axis=1, tiled=True)
    return arrived.reshape(count_here, arrived.shape[1], arrived.shape[3])


def merged(block):
    return block.reshape(block.shape[0] * block.shape[1], block.shape[2], block.shape[3])


def local_factored(streams, taps, filters, cotangent):
    block_rows = streams.shape[1]
    tap_reach = taps.shape[1] - 1
    earlier = shifted(streams[:, block_rows - tap_reach :, :], "ctx", 1)
    extended = jnp.concatenate([earlier, streams], axis=1).astype(jnp.float32)
    convolved = jnp.zeros((3, block_rows, streams.shape[2]), jnp.float32)
    for offset in range(tap_reach + 1):
        convolved = (
            convolved
            + taps[:, offset, None, :]
            * extended[:, tap_reach - offset : tap_reach - offset + block_rows, :]
        )
    query_side = convolved[0]
    key_side = convolved[1]
    value_side = convolved[2]
    product = (key_side * value_side).astype(jnp.bfloat16)
    seq_total = block_rows * lax.axis_size("ctx")
    scale_factor = 1.0 / math.sqrt(seq_total)
    arrived = regroup_out(jnp.stack([product, filters]).swapaxes(1, 2))
    per_stream = arrived.shape[1]
    grid_rows = arrived.shape[2]
    first_re, first_im = forward_transform(merged(arrived))
    prod_re = first_re[:per_stream]
    prod_im = first_im[:per_stream]
    filt_re = first_re[per_stream:]
    filt_im = first_im[per_stream:]
    mixed_re = prod_re * filt_re - prod_im * filt_im
    mixed_im = prod_re * filt_im + prod_im * filt_re
    mixed_cols = inverse_transform(mixed_re, mixed_im, grid_rows).astype(jnp.bfloat16)
    mixed_back = regroup_back(mixed_cols.reshape(1, per_stream, grid_rows, mixed_cols.shape[2]))
    mixed = mixed_back[0].T.astype(jnp.float32)
    gated = (query_side * mixed).astype(jnp.bfloat16)
    upstream = cotangent.astype(jnp.float32)
    mixed_grad = (upstream * query_side).astype(jnp.bfloat16)
    query_grad = upstream * mixed
    grad_cols = regroup_out(mixed_grad.T[None])
    grad_re, grad_im = forward_transform(merged(grad_cols))
    through_re = filt_re * grad_re + filt_im * grad_im
    through_im = filt_re * grad_im - filt_im * grad_re
    lagged_re = prod_re * grad_re + prod_im * grad_im
    lagged_im = prod_re * grad_im - prod_im * grad_re
    both_times = inverse_transform(
        jnp.concatenate([through_re, lagged_re], axis=0),
        jnp.concatenate([through_im, lagged_im], axis=0),
        grid_rows,
    )
    product_grad_cols = both_times[:per_stream].astype(jnp.bfloat16)
    filter_grad_cols = (both_times[per_stream:] * scale_factor).astype(jnp.bfloat16)
    returned = regroup_back(jnp.stack([product_grad_cols, filter_grad_cols]))
    product_grad = returned[0].T.astype(jnp.float32)
    filter_grad = returned[1].T
    conv_grad = jnp.stack([query_grad, product_grad * value_side, product_grad * key_side])
    following = shifted(conv_grad[:, :tap_reach, :].astype(jnp.bfloat16), "ctx", -1).astype(
        jnp.float32
    )
    extended_grad = jnp.concatenate([conv_grad, following], axis=1)
    running = jnp.zeros((3, block_rows, streams.shape[2]), jnp.float32)
    for offset in range(tap_reach + 1):
        running = (
            running + taps[:, offset, None, :] * extended_grad[:, offset : offset + block_rows, :]
        )
    stream_grad = running.astype(jnp.bfloat16)
    tap_terms = jnp.stack(
        [
            jnp.sum(
                conv_grad * extended[:, tap_reach - offset : tap_reach - offset + block_rows, :],
                axis=1,
            )
            for offset in range(tap_reach + 1)
        ],
        axis=1,
    )
    tap_grad = lax.psum(tap_terms, "ctx") * scale_factor
    return (gated, stream_grad, filter_grad, tap_grad)


def local(streams, taps, filters, cotangent):
    count = lax.axis_size("ctx")
    rows, channels = filters.shape
    tap_count = taps.shape[1]
    pairs_fill_lanes = channels == count * HALF and count % 2 == 0
    short_enough = rows % LANES == 0 and 3 * (rows * count) ** 2 <= TABLE_BYTES and tap_count < EDGE
    if pairs_fill_lanes and short_enough:
        return local_dense(streams, taps, filters, cotangent)
    return local_factored(streams, taps, filters, cotangent)


def solution(mesh):
    in_specs = (P(None, "ctx", "fft"), P(None, None, "fft"), P("ctx", "fft"), P("ctx", "fft"))
    out_specs = (P("ctx", "fft"), P(None, "ctx", "fft"), P("ctx", "fft"), P(None, None, "fft"))
    return jax.shard_map(local, mesh=mesh, in_specs=in_specs, out_specs=out_specs, check_vma=False)
```

```python
import functools
import math

import jax
import jax.numpy as jnp
import numpy as np
from jax import lax
from jax.experimental import pallas as pl
from jax.experimental.pallas import tpu as pltpu
from jax.sharding import PartitionSpec as P

exact_mode = lax.Precision.HIGHEST
LANES = 128
HALF = LANES // 2
PHASES = 4
EDGE = 8
ROW_TILE = 16
TABLE_BYTES = 16 * 1024 * 1024
VMEM_BYTES = 32 * 1024 * 1024


def step_offsets(count):
    groups = count // 2
    far = groups // 2
    near = [g for g in range(1, groups) if g != far]
    order = [(g, 0) for g in near[:1]] + [(far, 0)] + [(g, 1) for g in near[:1]] + [(far, 1)]
    order = order + [(g, 1) for g in near[1:]] + [(0, 1)] + [(g, 0) for g in near[1:]]
    return [(0, 0)] + [offset for offset in order if offset != (0, 0)]


def partner(index, offset, sign, count):
    group, member = offset
    groups = count // 2
    moved = (index // 2 + sign * group + groups) % groups
    flipped = (index + member) % 2
    return moved * 2 + flipped


def lower_lanes(rows):
    return lax.broadcasted_iota(jnp.int32, (rows, LANES), 1) < HALF


def turned(value):
    return pltpu.roll(value, HALF, 1)


def wide(value):
    return value.astype(jnp.float32)


def paired(first, second, odd, low):
    left = pltpu.roll(first, odd * HALF, 1)
    right = pltpu.roll(second, HALF - odd * HALF, 1)
    return jnp.where(low, left, right).astype(jnp.bfloat16)


def pack_kernel(count, *refs):
    streams_hbm, filters_hbm, cotangent_hbm, taps_hbm = refs[:4]
    out_refs = refs[4 : 5 + count]
    streams_ref, filters_ref, cotangent_ref, taps_ref, sems = refs[5 + count :]
    me = lax.axis_index("ctx")
    offsets = step_offsets(count)
    rows = filters_ref.shape[0]
    half_rows = rows // 2
    tap_count = taps_ref.shape[1]
    low = lower_lanes(rows)
    low_half = lower_lanes(half_rows)
    moves = (
        (filters_hbm, filters_ref), (streams_hbm.at[1:], streams_ref.at[1:]), (streams_hbm.at[:1], streams_ref.at[:1]),
        (cotangent_hbm, cotangent_ref), (taps_hbm, taps_ref),
    )
    copies = [pltpu.make_async_copy(here, there, sems.at[k]) for k, (here, there) in enumerate(moves)]
    for copy in copies:
        copy.start()

    def place(owner):
        return pl.ds(pl.multiple_of(owner // 2 * LANES, LANES), LANES), lax.rem(owner, 2)

    places = [place(partner(me, offsets[step], 1, count)) for step in range(count)]
    copies[0].wait()
    for (cols, odd), out in zip(places, out_refs):
        lag_block = wide(filters_ref[:, cols])
        out[2 * rows :, :] = paired(lag_block[:half_rows], lag_block[half_rows:], odd, low_half)
    copies[1].wait()
    for (cols, odd), out in zip(places, out_refs):
        out[0:rows, :] = paired(wide(streams_ref[1, :, cols]), wide(streams_ref[2, :, cols]), odd, low)
    copies[2].wait()
    copies[3].wait()
    for (cols, odd), out in zip(places, out_refs):
        out[rows : 2 * rows, :] = paired(wide(streams_ref[0, :, cols]), wide(cotangent_ref[:, cols]), odd, low)
    copies[4].wait()
    cols, odd = place(me)
    tap_out = out_refs[count]
    low_taps = lower_lanes(tap_count)
    here = [pltpu.roll(taps_ref[i, :, cols], odd * HALF, 1) for i in range(3)]
    first_tap = lax.broadcasted_iota(jnp.int32, (tap_count, LANES), 0) == 0
    tap_out[...] = jnp.zeros_like(tap_out)
    tap_out[0:tap_count, :] = jnp.where(low_taps, here[1], turned(here[2]))
    tap_out[EDGE : EDGE + tap_count, :] = jnp.where(low_taps, here[0], jnp.where(first_tap, 1.0, 0.0))


def phase_tables(total):
    quarter = total // PHASES
    freq = 2 * np.arange(quarter)[:, None] + 1
    ahead, back = [], []
    for phase in range(PHASES):
        place = PHASES * np.arange(quarter)[None, :] + phase
        angles = (freq * place % (4 * total)) * (math.pi / (2 * total))
        table = np.concatenate([np.cos(angles), -np.sin(angles)])
        ahead.append(table)
        back.append(table.T / total)
    ahead = np.stack(ahead)
    high = ahead.astype(jnp.bfloat16)
    rest = (ahead - high.astype(np.float64)).astype(jnp.bfloat16)
    return high, rest, np.stack(back).astype(jnp.bfloat16)


def quarter_turns(parts):
    (r0, i0), (r1, i1), (r2, i2), (r3, i3) = parts
    even_r, even_i, odd_r, odd_i = r0 + r2, i0 + i2, r1 + r3, i1 + i3
    gap_r, gap_i, side_r, side_i = r0 - r2, i0 - i2, r1 - r3, i1 - i3
    return [
        (even_r + odd_r, even_i + odd_i),
        (gap_r - side_i, gap_i + side_r),
        (even_r - odd_r, even_i - odd_i),
        (gap_r + side_i, gap_i - side_r),
    ]


def main_kernel(count, tap_count, scale, *refs):
    in_refs = refs[:count]
    tap_ref, high, rest, back = refs[count : count + 4]
    out_refs = refs[count + 4 : 2 * count + 4]
    (raw_kv, raw_qc, raw_lag, conv_kv, conv_qc, signals, phased, spectra, pairs, grad_kv, grad_q, lag_grad, extra) = refs[
        2 * count + 4 :
    ]
    me = lax.axis_index("ctx")
    offsets = step_offsets(count)
    total = raw_lag.shape[0]
    quarter = total // PHASES
    rows = total // count
    half_rows = rows // 2
    low_half = lower_lanes(half_rows)

    raw_kv[0:EDGE, :] = jnp.zeros((EDGE, LANES), jnp.float32)
    raw_qc[0:EDGE, :] = jnp.zeros((EDGE, LANES), jnp.float32)
    grad_kv[total:, :] = jnp.zeros((EDGE, LANES), jnp.float32)
    grad_q[total:, :] = jnp.zeros((EDGE, LANES), jnp.float32)
    for step in range(count):
        source = partner(me, offsets[step], -1, count)
        base = pl.multiple_of(source * rows, rows)
        block = in_refs[step]
        raw_kv[pl.ds(base + EDGE, rows), :] = wide(block[0:rows, :])
        raw_qc[pl.ds(base + EDGE, rows), :] = wide(block[rows : 2 * rows, :])
        lag_block = wide(block[2 * rows :, :])
        other = turned(lag_block)
        raw_lag[pl.ds(base, half_rows), :] = jnp.where(low_half, lag_block, other)
        raw_lag[pl.ds(base + half_rows, half_rows), :] = jnp.where(low_half, other, lag_block)

    tap_kv = [tap_ref[j : j + 1, :] for j in range(tap_count)]
    tap_q = [tap_ref[EDGE + j : EDGE + j + 1, :] for j in range(tap_count)]

    part = min(32, quarter)
    low = lower_lanes(part)
    for start in range(0, quarter, part):
        for phase in range(PHASES):
            first = PHASES * start + phase
            here = slice(phase * quarter + start, phase * quarter + start + part)
            key_value = jnp.zeros((part, LANES), jnp.float32)
            query_cot = jnp.zeros((part, LANES), jnp.float32)
            for j in range(tap_count):
                window = pl.ds(first + EDGE - j, part, stride=PHASES)
                key_value = key_value + tap_kv[j] * raw_kv[window, :]
                query_cot = query_cot + tap_q[j] * raw_qc[window, :]
            conv_kv[here, :] = key_value
            conv_qc[here, :] = query_cot
            product = key_value * turned(key_value)
            mixed_grad = query_cot * turned(query_cot)
            signals[here, :LANES] = jnp.where(low, product, mixed_grad).astype(jnp.bfloat16)
            signals[here, LANES:] = raw_lag[pl.ds(first, part, stride=PHASES), :].astype(jnp.bfloat16)

    for phase in range(PHASES):
        signal = signals[phase * quarter : (phase + 1) * quarter, :]
        phased[phase, :, :] = jnp.dot(high[phase], signal, preferred_element_type=jnp.float32) + jnp.dot(
            rest[phase], signal, preferred_element_type=jnp.float32
        )

    part = min(16, quarter)
    low = lower_lanes(part)
    for start in range(0, quarter, part):
        real, imag = slice(start, start + part), slice(quarter + start, quarter + start + part)
        signal_turns = quarter_turns([(phased[p, real, :LANES], phased[p, imag, :LANES]) for p in range(PHASES)])
        lag_turns = quarter_turns([(phased[p, real, LANES:], phased[p, imag, LANES:]) for p in range(PHASES)])
        through, lagged = [], []
        for (a_re, a_im), (b_re, b_im) in zip(signal_turns, lag_turns):
            b_im = jnp.where(low, b_im, -b_im)
            r_re, r_im = turned(a_re), turned(a_im)
            through.append((a_re * b_re - a_im * b_im, a_re * b_im + a_im * b_re))
            lagged.append((a_re * r_re + a_im * r_im, a_re * r_im - a_im * r_re))
        for cols, parts in ((slice(0, LANES), through), (slice(LANES, 2 * LANES), lagged)):
            turns = quarter_turns(parts)
            for phase in range(PHASES):
                value_re, value_im = turns[-phase % PHASES]
                spectra[phase, real, cols] = value_re.astype(jnp.bfloat16)
                spectra[phase, imag, cols] = value_im.astype(jnp.bfloat16)

    low = lower_lanes(quarter)
    for phase in range(PHASES):
        here = slice(phase * quarter, (phase + 1) * quarter)
        spread = pl.ds(phase, quarter, stride=PHASES)
        result = jnp.dot(back[phase], spectra[phase], preferred_element_type=jnp.float32)
        pair = wide(result[:, :LANES].astype(jnp.bfloat16))
        other = turned(pair)
        pairs[spread, :] = pair
        grad_q[spread, :] = turned(conv_qc[here, :]) * jnp.where(low, pair, other)
        grad_kv[spread, :] = jnp.where(low, other, pair) * turned(conv_kv[here, :])
        lag_grad[spread, :] = result[:, LANES:] * scale

    extra[...] = jnp.zeros_like(extra)
    tap_sum_kv = [jnp.zeros((EDGE, LANES), jnp.float32)] * tap_count
    tap_sum_q = [jnp.zeros((EDGE, LANES), jnp.float32)] * tap_count
    part = min(32, rows)
    for base in range(0, total, part):
        kv = grad_kv[base : base + part, :]
        q = grad_q[base : base + part, :]
        for j in range(tap_count):
            window = slice(base + EDGE - j, base + EDGE - j + part)
            tap_sum_kv[j] = tap_sum_kv[j] + jnp.sum((kv * raw_kv[window, :]).reshape(part // EDGE, EDGE, LANES), axis=0)
            tap_sum_q[j] = tap_sum_q[j] + jnp.sum((q * raw_qc[window, :]).reshape(part // EDGE, EDGE, LANES), axis=0)
    spare = [jnp.zeros((1, LANES), jnp.float32)] * (EDGE - tap_count)
    sums = [
        jnp.concatenate([jnp.sum(s, axis=0, keepdims=True) for s in parts] + spare, axis=0) * scale
        for parts in (tap_sum_kv, tap_sum_q)
    ]
    reach = tap_count - 1
    low_taps, low_reach = lower_lanes(tap_count), lower_lanes(reach)
    sums_kv, sums_q = [s[:tap_count] for s in sums]
    high_q = wide(sums_q.astype(jnp.bfloat16))
    extra[3 * reach : 3 * reach + tap_count, :] = sums_kv
    extra[3 * reach + tap_count : 3 * reach + 2 * tap_count, :] = jnp.where(low_taps, high_q, turned(sums_q - high_q))
    for step in range(count):
        owner = partner(me, offsets[step], 1, count)
        base = pl.multiple_of(owner * rows, rows)
        out = out_refs[step]
        out[0:rows, :] = pairs[pl.ds(base, rows), :].astype(jnp.bfloat16)
        out[rows : rows + half_rows, :] = jnp.where(
            low_half, lag_grad[pl.ds(base, half_rows), :], turned(lag_grad[pl.ds(base + half_rows, half_rows), :])
        ).astype(jnp.bfloat16)
        extra[0:reach, :] = raw_kv[pl.ds(base + EDGE - reach, reach), :]
        extra[reach : 2 * reach, :] = grad_kv[pl.ds(base + rows, reach), :]
        extra[2 * reach : 3 * reach, :] = jnp.where(
            low_reach, raw_qc[pl.ds(base + EDGE - reach, reach), :], turned(grad_q[pl.ds(base + rows, reach), :])
        )
        out[rows + half_rows :, :] = extra[...].astype(jnp.bfloat16)


def shifted_sum(taps, padded, first, direction, rows):
    return sum(taps[j] * padded[first + direction * j : first + direction * j + rows, :] for j in range(len(taps)))


def local_kernel(tap_count, streams_hbm, taps_hbm, cotangent_hbm, high_hbm, rest_hbm, back_hbm, arrived_ref, *refs):
    conv_ref, taps_ref, cotangent_ref, high_ref, rest_ref, back_ref, streams_ref, padded, sems = refs
    pairs = (
        (streams_hbm, streams_ref), (taps_hbm, taps_ref), (cotangent_hbm, cotangent_ref),
        (high_hbm, high_ref), (rest_hbm, rest_ref), (back_hbm, back_ref),
    )
    copies = [pltpu.make_async_copy(here, there, sems.at[k]) for k, (here, there) in enumerate(pairs)]
    for copy in copies:
        copy.start()
    copies[0].wait()
    copies[1].wait()
    streams, rows, channels = conv_ref.shape
    padded[0:EDGE, :] = jnp.zeros((EDGE, LANES), jnp.float32)
    for i in range(streams):
        for start in range(0, channels, LANES):
            cols = slice(start, start + LANES)
            padded[EDGE:, :] = wide(streams_ref[i, :, cols])
            taps = [taps_ref[i, j : j + 1, cols] for j in range(tap_count)]
            conv_ref[i, :, cols] = shifted_sum(taps, padded, EDGE, -1, rows)
    for copy in copies[2:]:
        copy.wait()


def finish_kernel(count, tap_count, *refs):
    in_refs = refs[:count]
    conv_ref, taps_ref, cotangent_ref = refs[count : count + 3]
    out_hbm = refs[count + 3 : count + 7]
    gated_ref, stream_ref, lag_ref, tap_ref, blocks, extras, edges, grads, sems, tap_sem = refs[count + 7 :]
    me = lax.axis_index("ctx")
    offsets = step_offsets(count)
    rows = gated_ref.shape[0]
    half_rows = rows // 2
    reach = tap_count - 1
    low = lower_lanes(rows)
    low_half = lower_lanes(half_rows)
    low_extra = lower_lanes(extras.shape[1])
    low_taps = lower_lanes(tap_count)
    for step in range(count):
        owner = partner(me, offsets[step], -1, count)
        blocks[owner, :, :] = in_refs[step][...]
    edges[...] = jnp.zeros_like(edges)
    copies = []
    for pair in range(count // 2):
        cols = slice(pair * LANES, (pair + 1) * LANES)

        def both(window, mask):
            even, odd = wide(blocks[2 * pair, window, :]), wide(blocks[2 * pair + 1, window, :])
            return jnp.where(mask, even, turned(odd)), jnp.where(mask, turned(even), odd)

        extra_rows = slice(rows + half_rows, None)
        extras[0, :, :], extras[1, :, :] = both(extra_rows, low_extra)
        mixed, product_grad = both(slice(0, rows), low)
        lag_lower, lag_upper = both(slice(rows, rows + half_rows), low_half)
        lag_ref[0:half_rows, cols] = lag_lower.astype(jnp.bfloat16)
        lag_ref[half_rows:, cols] = lag_upper.astype(jnp.bfloat16)
        taps = [[taps_ref[i, j : j + 1, cols] for j in range(tap_count)] for i in range(3)]
        befores = (extras[0, 2 * reach : 3 * reach, :], extras[0, 0:reach, :], extras[1, 0:reach, :])
        afters = (extras[1, 2 * reach : 3 * reach, :], extras[0, reach : 2 * reach, :], extras[1, reach : 2 * reach, :])
        convolved = []
        for i in range(3):
            edges[i, EDGE - reach : EDGE, :] = befores[i]
            first = conv_ref[i, 0:EDGE, cols] + shifted_sum(taps[i], edges.at[i], EDGE, -1, EDGE)
            convolved.append(jnp.concatenate([first, conv_ref[i, EDGE:, cols]], axis=0))
        query, key, value = convolved
        gated_ref[:, cols] = (query * mixed).astype(jnp.bfloat16)
        own = (wide(cotangent_ref[:, cols]) * mixed, product_grad * value, product_grad * key)
        for i in range(3):
            grads[i, 0:rows, :] = own[i]
            grads[i, rows : rows + reach, :] = afters[i]
            stream_ref[i, :, cols] = shifted_sum(taps[i], grads.at[i], 0, 1, rows).astype(jnp.bfloat16)
        sums_kv = slice(3 * reach, 3 * reach + tap_count)
        sums_q = slice(3 * reach + tap_count, 3 * reach + 2 * tap_count)
        tap_ref[1, :, cols] = extras[0, sums_kv, :]
        tap_ref[2, :, cols] = extras[1, sums_kv, :]
        tap_ref[0, :, cols] = extras[0, sums_q, :] + extras[1, sums_q, :]
        held = (gated_ref.at[:, cols], stream_ref.at[:, :, cols], lag_ref.at[:, cols])
        there = (out_hbm[0].at[:, cols], out_hbm[1].at[:, :, cols], out_hbm[2].at[:, cols])
        for k in range(3):
            copies.append(pltpu.make_async_copy(held[k], there[k], sems.at[pair, k]))
            copies[-1].start()
    copies.append(pltpu.make_async_copy(tap_ref, out_hbm[3], tap_sem.at[0]))
    copies[-1].start()
    for copy in copies:
        copy.wait()


def exchanged(blocks):
    count = len(blocks)
    return [blocks[0]] + [
        lax.ppermute(block, "ctx", [(source, partner(source, offset, 1, count)) for source in range(count)])
        for block, offset in zip(blocks[1:], step_offsets(count)[1:])
    ]


def in_hbm(array):
    return pltpu.with_memory_space_constraint(array, pltpu.HBM)


def in_vmem(count):
    return [pl.BlockSpec(memory_space=pltpu.VMEM)] * count


def local_dense(streams, taps, filters, cotangent):
    count = lax.axis_size("ctx")
    rows, channels = filters.shape
    tap_count = taps.shape[1]
    total = rows * count
    params = pltpu.CompilerParams(vmem_limit_bytes=VMEM_BYTES)
    sent_rows = 2 * rows + rows // 2
    packed = pl.pallas_call(
        functools.partial(pack_kernel, count),
        out_shape=[jax.ShapeDtypeStruct((sent_rows, LANES), jnp.bfloat16)] * count
        + [jax.ShapeDtypeStruct((2 * EDGE, LANES), jnp.float32)],
        in_specs=[pl.BlockSpec(memory_space=pltpu.HBM)] * 4,
        out_specs=in_vmem(count + 1),
        scratch_shapes=[pltpu.VMEM(a.shape, a.dtype) for a in (streams, filters, cotangent, taps)]
        + [pltpu.SemaphoreType.DMA((5,))],
        compiler_params=params,
        name="pack",
    )(*[in_hbm(a) for a in (streams, filters, cotangent, taps)])
    arrived = exchanged(packed[:count])
    quarter = total // PHASES
    tables = phase_tables(total)
    hbm = pl.BlockSpec(memory_space=pltpu.HBM)
    conv, taps_here, cotangent_here, *tables_here = pl.pallas_call(
        functools.partial(local_kernel, tap_count),
        out_shape=[
            jax.ShapeDtypeStruct(streams.shape, jnp.float32),
            jax.ShapeDtypeStruct(taps.shape, taps.dtype),
            jax.ShapeDtypeStruct(cotangent.shape, cotangent.dtype),
            *[jax.ShapeDtypeStruct(table.shape, jnp.bfloat16) for table in tables],
        ],
        in_specs=[hbm] * (3 + len(tables)) + [pl.BlockSpec(memory_space=pl.ANY)],
        out_specs=in_vmem(3 + len(tables)),
        scratch_shapes=[
            pltpu.VMEM(streams.shape, streams.dtype),
            pltpu.VMEM((rows + EDGE, LANES), jnp.float32),
            pltpu.SemaphoreType.DMA((3 + len(tables),)),
        ],
        compiler_params=params,
        name="local",
    )(*[in_hbm(jnp.asarray(a)) for a in (streams, taps, cotangent, *tables)], arrived[count - 2])
    extra_rows = -(-(5 * tap_count - 3) // ROW_TILE) * ROW_TILE
    back_rows = rows + rows // 2 + extra_rows
    f32_rows = lambda extent: pltpu.VMEM((extent, LANES), jnp.float32)
    made = pl.pallas_call(
        functools.partial(main_kernel, count, tap_count, 1.0 / math.sqrt(total)),
        out_shape=[jax.ShapeDtypeStruct((back_rows, LANES), jnp.bfloat16)] * count,
        in_specs=in_vmem(count + 1 + len(tables)),
        out_specs=in_vmem(count),
        scratch_shapes=[
            f32_rows(total + EDGE), f32_rows(total + EDGE), f32_rows(total), f32_rows(total), f32_rows(total),
            pltpu.VMEM((total, 2 * LANES), jnp.bfloat16),
            pltpu.VMEM((PHASES, 2 * quarter, 2 * LANES), jnp.float32),
            pltpu.VMEM((PHASES, 2 * quarter, 2 * LANES), jnp.bfloat16),
            f32_rows(total), f32_rows(total + EDGE), f32_rows(total + EDGE), f32_rows(total), f32_rows(extra_rows),
        ],
        compiler_params=params,
        name="channels",
    )(*arrived, packed[count], *tables_here)
    returned = exchanged(made)
    outs = [
        jax.ShapeDtypeStruct(filters.shape, jnp.bfloat16),
        jax.ShapeDtypeStruct(streams.shape, jnp.bfloat16),
        jax.ShapeDtypeStruct(filters.shape, jnp.bfloat16),
        jax.ShapeDtypeStruct(taps.shape, jnp.float32),
    ]
    return tuple(
        pl.pallas_call(
            functools.partial(finish_kernel, count, tap_count),
            out_shape=outs,
            in_specs=in_vmem(count + 3),
            out_specs=[hbm] * len(outs),
            scratch_shapes=[pltpu.VMEM(out.shape, out.dtype) for out in outs]
            + [
                pltpu.VMEM((count, back_rows, LANES), jnp.bfloat16),
                pltpu.VMEM((2, extra_rows, LANES), jnp.float32),
                pltpu.VMEM((3, 2 * EDGE, LANES), jnp.float32),
                pltpu.VMEM((3, rows + EDGE, LANES), jnp.float32),
                pltpu.SemaphoreType.DMA((count // 2, 3)),
                pltpu.SemaphoreType.DMA((1,)),
            ],
            compiler_params=params,
            name="finish",
        )(*returned, conv, taps_here, cotangent_here)
    )


def shifted(value, axis, steps):
    count = lax.axis_size(axis)
    first, last = (max(0, -steps), min(count, count - steps))
    return lax.ppermute(value, axis, [(source, source + steps) for source in range(first, last)])


def angle_table(row_count, col_count, col_start, period):
    row_ids = lax.iota(jnp.int32, row_count)
    col_ids = col_start + lax.iota(jnp.int32, col_count)
    turns = row_ids[:, None] * col_ids[None, :] % period
    angles = turns.astype(jnp.float32) * (2.0 * math.pi / period)
    return (jnp.cos(angles), jnp.sin(angles))


def column_start():
    return 0


def split_product(table, signal):
    high_part = table.astype(jnp.bfloat16)
    low_part = (table - high_part.astype(jnp.float32)).astype(jnp.bfloat16)
    first = jnp.einsum("kt,ctu->cku", high_part, signal, preferred_element_type=jnp.float32)
    second = jnp.einsum("kt,ctu->cku", low_part, signal, preferred_element_type=jnp.float32)
    return first + second


def forward_transform(signal):
    input_rows = signal.shape[1]
    row_count = 2 * input_rows
    col_count = signal.shape[2]
    period = row_count * col_count
    cos_first, sin_first = angle_table(row_count, input_rows, 0, row_count)
    first_re = split_product(cos_first, signal)
    first_im = -split_product(sin_first, signal)
    cos_twist, sin_twist = angle_table(row_count, col_count, column_start(), period)
    turned_re = first_re * cos_twist + first_im * sin_twist
    turned_im = first_im * cos_twist - first_re * sin_twist
    cos_second, sin_second = angle_table(col_count, col_count, 0, col_count)
    spec_re = jnp.einsum("cut,tk->cuk", turned_re, cos_second, precision=exact_mode) + jnp.einsum(
        "cut,tk->cuk", turned_im, sin_second, precision=exact_mode
    )
    spec_im = jnp.einsum("cut,tk->cuk", turned_im, cos_second, precision=exact_mode) - jnp.einsum(
        "cut,tk->cuk", turned_re, sin_second, precision=exact_mode
    )
    return (spec_re, spec_im)


def inverse_transform(spec_re, spec_im, keep_rows):
    full_width = spec_re.shape[2]
    cos_second, sin_second = angle_table(full_width, full_width, 0, full_width)
    back_re = jnp.einsum("cuk,kt->cut", spec_re, cos_second, precision=exact_mode) - jnp.einsum(
        "cuk,kt->cut", spec_im, sin_second, precision=exact_mode
    )
    back_im = jnp.einsum("cuk,kt->cut", spec_im, cos_second, precision=exact_mode) + jnp.einsum(
        "cuk,kt->cut", spec_re, sin_second, precision=exact_mode
    )
    row_count = back_re.shape[1]
    col_count = back_re.shape[2]
    period = row_count * full_width
    cos_twist, sin_twist = angle_table(row_count, col_count, column_start(), period)
    turned_re = back_re * cos_twist - back_im * sin_twist
    turned_im = back_im * cos_twist + back_re * sin_twist
    cos_first, sin_first = angle_table(keep_rows, row_count, 0, row_count)
    result = jnp.einsum("tk,cku->ctu", cos_first, turned_re, precision=exact_mode) - jnp.einsum(
        "tk,cku->ctu", sin_first, turned_im, precision=exact_mode
    )
    return result * (1.0 / period)


def regroup_out(stacked):
    count_here = stacked.shape[0]
    channel_count = stacked.shape[1]
    block_rows = stacked.shape[2]
    shaped = stacked.reshape(count_here, channel_count, 1, block_rows)
    return lax.all_to_all(shaped, "ctx", split_axis=1, concat_axis=2, tiled=True)


def regroup_back(stacked):
    count_here = stacked.shape[0]
    arrived = lax.all_to_all(stacked, "ctx", split_axis=2, concat_axis=1, tiled=True)
    return arrived.reshape(count_here, arrived.shape[1], arrived.shape[3])


def merged(block):
    return block.reshape(block.shape[0] * block.shape[1], block.shape[2], block.shape[3])


def local_factored(streams, taps, filters, cotangent):
    block_rows = streams.shape[1]
    tap_reach = taps.shape[1] - 1
    earlier = shifted(streams[:, block_rows - tap_reach :, :], "ctx", 1)
    extended = jnp.concatenate([earlier, streams], axis=1).astype(jnp.float32)
    convolved = jnp.zeros((3, block_rows, streams.shape[2]), jnp.float32)
    for offset in range(tap_reach + 1):
        convolved = (
            convolved
            + taps[:, offset, None, :]
            * extended[:, tap_reach - offset : tap_reach - offset + block_rows, :]
        )
    query_side = convolved[0]
    key_side = convolved[1]
    value_side = convolved[2]
    product = (key_side * value_side).astype(jnp.bfloat16)
    seq_total = block_rows * lax.axis_size("ctx")
    scale_factor = 1.0 / math.sqrt(seq_total)
    arrived = regroup_out(jnp.stack([product, filters]).swapaxes(1, 2))
    per_stream = arrived.shape[1]
    grid_rows = arrived.shape[2]
    first_re, first_im = forward_transform(merged(arrived))
    prod_re = first_re[:per_stream]
    prod_im = first_im[:per_stream]
    filt_re = first_re[per_stream:]
    filt_im = first_im[per_stream:]
    mixed_re = prod_re * filt_re - prod_im * filt_im
    mixed_im = prod_re * filt_im + prod_im * filt_re
    mixed_cols = inverse_transform(mixed_re, mixed_im, grid_rows).astype(jnp.bfloat16)
    mixed_back = regroup_back(mixed_cols.reshape(1, per_stream, grid_rows, mixed_cols.shape[2]))
    mixed = mixed_back[0].T.astype(jnp.float32)
    gated = (query_side * mixed).astype(jnp.bfloat16)
    upstream = cotangent.astype(jnp.float32)
    mixed_grad = (upstream * query_side).astype(jnp.bfloat16)
    query_grad = upstream * mixed
    grad_cols = regroup_out(mixed_grad.T[None])
    grad_re, grad_im = forward_transform(merged(grad_cols))
    through_re = filt_re * grad_re + filt_im * grad_im
    through_im = filt_re * grad_im - filt_im * grad_re
    lagged_re = prod_re * grad_re + prod_im * grad_im
    lagged_im = prod_re * grad_im - prod_im * grad_re
    both_times = inverse_transform(
        jnp.concatenate([through_re, lagged_re], axis=0),
        jnp.concatenate([through_im, lagged_im], axis=0),
        grid_rows,
    )
    product_grad_cols = both_times[:per_stream].astype(jnp.bfloat16)
    filter_grad_cols = (both_times[per_stream:] * scale_factor).astype(jnp.bfloat16)
    returned = regroup_back(jnp.stack([product_grad_cols, filter_grad_cols]))
    product_grad = returned[0].T.astype(jnp.float32)
    filter_grad = returned[1].T
    conv_grad = jnp.stack([query_grad, product_grad * value_side, product_grad * key_side])
    following = shifted(conv_grad[:, :tap_reach, :].astype(jnp.bfloat16), "ctx", -1).astype(
        jnp.float32
    )
    extended_grad = jnp.concatenate([conv_grad, following], axis=1)
    running = jnp.zeros((3, block_rows, streams.shape[2]), jnp.float32)
    for offset in range(tap_reach + 1):
        running = (
            running + taps[:, offset, None, :] * extended_grad[:, offset : offset + block_rows, :]
        )
    stream_grad = running.astype(jnp.bfloat16)
    tap_terms = jnp.stack(
        [
            jnp.sum(
                conv_grad * extended[:, tap_reach - offset : tap_reach - offset + block_rows, :],
                axis=1,
            )
            for offset in range(tap_reach + 1)
        ],
        axis=1,
    )
    tap_grad = lax.psum(tap_terms, "ctx") * scale_factor
    return (gated, stream_grad, filter_grad, tap_grad)


def local(streams, taps, filters, cotangent):
    count = lax.axis_size("ctx")
    rows, channels = filters.shape
    tap_count = taps.shape[1]
    pairs_fill_lanes = channels == count * HALF and count % 2 == 0
    short_enough = rows % LANES == 0 and 3 * (rows * count) ** 2 <= TABLE_BYTES and tap_count < EDGE
    if pairs_fill_lanes and short_enough:
        return local_dense(streams, taps, filters, cotangent)
    return local_factored(streams, taps, filters, cotangent)


def solution(mesh):
    in_specs = (P(None, "ctx", "fft"), P(None, None, "fft"), P("ctx", "fft"), P("ctx", "fft"))
    out_specs = (P("ctx", "fft"), P(None, "ctx", "fft"), P("ctx", "fft"), P(None, None, "fft"))
    return jax.shard_map(local, mesh=mesh, in_specs=in_specs, out_specs=out_specs, check_vma=False)
```

```python
import functools
import math

import jax
import jax.numpy as jnp
import numpy as np
from jax import lax
from jax.experimental import pallas as pl
from jax.experimental.pallas import tpu as pltpu
from jax.sharding import PartitionSpec as P

exact_mode = lax.Precision.HIGHEST
LANES = 128
HALF = LANES // 2
PHASES = 4
EDGE = 8
ROW_TILE = 16
TABLE_BYTES = 16 * 1024 * 1024
VMEM_BYTES = 32 * 1024 * 1024


def step_offsets(count, back=False):
    groups = count // 2
    far = groups // 2
    near = [g for g in range(1, groups) if g != far]
    first, last = near[:1], near[1:]
    if back:
        order = [(far, 0)] + [(g, m) for g in first for m in (0, 1)] + [(far, 1)]
        order = order + [(g, 1) for g in last] + [(g, 0) for g in last] + [(0, 1)]
    else:
        order = [(far, 0), (0, 1), (far, 1)] + [(g, m) for g in first for m in (1, 0)]
        order = order + [(g, 1) for g in last] + [(g, 0) for g in last]
    return [(0, 0)] + [offset for offset in dict.fromkeys(order) if offset != (0, 0)]


def partner(index, offset, sign, count):
    group, member = offset
    groups = count // 2
    moved = (index // 2 + sign * group + groups) % groups
    flipped = (index + member) % 2
    return moved * 2 + flipped


def lower_lanes(rows):
    return lax.broadcasted_iota(jnp.int32, (rows, LANES), 1) < HALF


def turned(value):
    return pltpu.roll(value, HALF, 1)


def wide(value):
    return value.astype(jnp.float32)


def paired(first, second, odd, low):
    left = pltpu.roll(first, odd * HALF, 1)
    right = pltpu.roll(second, HALF - odd * HALF, 1)
    return jnp.where(low, left, right).astype(jnp.bfloat16)


def pack_kernel(count, *refs):
    streams_hbm, filters_hbm, cotangent_hbm, taps_hbm = refs[:4]
    out_refs = refs[4 : 5 + count]
    streams_ref, filters_ref, cotangent_ref, taps_ref, sems = refs[5 + count :]
    me = lax.axis_index("ctx")
    offsets = step_offsets(count)
    rows = filters_ref.shape[0]
    half_rows = rows // 2
    tap_count = taps_ref.shape[1]
    low = lower_lanes(rows)
    low_half = lower_lanes(half_rows)
    moves = (
        (filters_hbm, filters_ref), (streams_hbm.at[1:], streams_ref.at[1:]), (streams_hbm.at[:1], streams_ref.at[:1]),
        (cotangent_hbm, cotangent_ref), (taps_hbm, taps_ref),
    )
    copies = [pltpu.make_async_copy(here, there, sems.at[k]) for k, (here, there) in enumerate(moves)]
    for copy in copies:
        copy.start()

    def place(owner):
        return pl.ds(pl.multiple_of(owner // 2 * LANES, LANES), LANES), lax.rem(owner, 2)

    places = [place(partner(me, offsets[step], 1, count)) for step in range(count)]
    copies[0].wait()
    for (cols, odd), out in zip(places, out_refs):
        lag_block = wide(filters_ref[:, cols])
        out[2 * rows :, :] = paired(lag_block[:half_rows], lag_block[half_rows:], odd, low_half)
    copies[1].wait()
    for (cols, odd), out in zip(places, out_refs):
        out[0:rows, :] = paired(wide(streams_ref[1, :, cols]), wide(streams_ref[2, :, cols]), odd, low)
    copies[2].wait()
    copies[3].wait()
    for (cols, odd), out in zip(places, out_refs):
        out[rows : 2 * rows, :] = paired(wide(streams_ref[0, :, cols]), wide(cotangent_ref[:, cols]), odd, low)
    copies[4].wait()
    cols, odd = place(me)
    tap_out = out_refs[count]
    low_taps = lower_lanes(tap_count)
    here = [pltpu.roll(taps_ref[i, :, cols], odd * HALF, 1) for i in range(3)]
    first_tap = lax.broadcasted_iota(jnp.int32, (tap_count, LANES), 0) == 0
    tap_out[...] = jnp.zeros_like(tap_out)
    tap_out[0:tap_count, :] = jnp.where(low_taps, here[1], turned(here[2]))
    tap_out[EDGE : EDGE + tap_count, :] = jnp.where(low_taps, here[0], jnp.where(first_tap, 1.0, 0.0))


def phase_tables(total):
    quarter = total // PHASES
    freq = 2 * np.arange(quarter)[:, None] + 1
    ahead, back = [], []
    for phase in range(PHASES):
        place = PHASES * np.arange(quarter)[None, :] + phase
        angles = (freq * place % (4 * total)) * (math.pi / (2 * total))
        table = np.concatenate([np.cos(angles), -np.sin(angles)])
        ahead.append(table)
        back.append(table.T / total)
    ahead = np.stack(ahead)
    high = ahead.astype(jnp.bfloat16)
    rest = (ahead - high.astype(np.float64)).astype(jnp.bfloat16)
    return high, rest, np.stack(back).astype(jnp.bfloat16)


def quarter_turns(parts):
    (r0, i0), (r1, i1), (r2, i2), (r3, i3) = parts
    even_r, even_i, odd_r, odd_i = r0 + r2, i0 + i2, r1 + r3, i1 + i3
    gap_r, gap_i, side_r, side_i = r0 - r2, i0 - i2, r1 - r3, i1 - i3
    return [
        (even_r + odd_r, even_i + odd_i),
        (gap_r - side_i, gap_i + side_r),
        (even_r - odd_r, even_i - odd_i),
        (gap_r + side_i, gap_i - side_r),
    ]


def main_kernel(count, tap_count, scale, *refs):
    in_refs = refs[:count]
    tap_ref, high, rest, back = refs[count : count + 4]
    out_refs = refs[count + 4 : 2 * count + 4]
    (raw_kv, raw_qc, raw_lag, conv_kv, conv_qc, signals, phased, spectra, pairs, grad_kv, grad_q, lag_grad, extra) = refs[
        2 * count + 4 :
    ]
    me = lax.axis_index("ctx")
    offsets, back_offsets = step_offsets(count), step_offsets(count, back=True)
    total = signals.shape[0]
    quarter = total // PHASES
    rows = total // count
    half_rows = rows // 2
    low_half = lower_lanes(half_rows)

    raw_kv[0:EDGE, :] = jnp.zeros((EDGE, LANES), jnp.float32)
    raw_qc[0:EDGE, :] = jnp.zeros((EDGE, LANES), jnp.float32)
    grad_kv[total:, :] = jnp.zeros((EDGE, LANES), jnp.float32)
    grad_q[total:, :] = jnp.zeros((EDGE, LANES), jnp.float32)
    for step in range(count):
        source = partner(me, offsets[step], -1, count)
        base = pl.multiple_of(source * rows, rows)
        block = in_refs[step]
        raw_kv[pl.ds(base + EDGE, rows), :] = wide(block[0:rows, :])
        raw_qc[pl.ds(base + EDGE, rows), :] = wide(block[rows : 2 * rows, :])
        lag_block = wide(block[2 * rows :, :])
        other = turned(lag_block)
        raw_lag[pl.ds(base, half_rows), :] = jnp.where(low_half, lag_block, other)
        raw_lag[pl.ds(base + half_rows, half_rows), :] = jnp.where(low_half, other, lag_block)

    tap_kv = [tap_ref[j : j + 1, :] for j in range(tap_count)]
    tap_q = [tap_ref[EDGE + j : EDGE + j + 1, :] for j in range(tap_count)]

    part = min(32, quarter)
    low = lower_lanes(part)
    for start in range(0, quarter, part):
        for phase in range(PHASES):
            first = PHASES * start + phase
            here = slice(phase * quarter + start, phase * quarter + start + part)
            key_value = jnp.zeros((part, LANES), jnp.float32)
            query_cot = jnp.zeros((part, LANES), jnp.float32)
            for j in range(tap_count):
                window = pl.ds(first + EDGE - j, part, stride=PHASES)
                key_value = key_value + tap_kv[j] * raw_kv[window, :]
                query_cot = query_cot + tap_q[j] * raw_qc[window, :]
            conv_kv[here, :] = key_value
            conv_qc[here, :] = query_cot
            product = key_value * turned(key_value)
            mixed_grad = query_cot * turned(query_cot)
            signals[here, :LANES] = jnp.where(low, product, mixed_grad).astype(jnp.bfloat16)
            signals[here, LANES:] = raw_lag[pl.ds(first, part, stride=PHASES), :].astype(jnp.bfloat16)

    for phase in range(PHASES):
        signal = signals[phase * quarter : (phase + 1) * quarter, :]
        phased[phase, :, :] = jnp.dot(high[phase], signal, preferred_element_type=jnp.float32) + jnp.dot(
            rest[phase], signal, preferred_element_type=jnp.float32
        )

    part = min(16, quarter)
    low = lower_lanes(part)
    for start in range(0, quarter, part):
        real, imag = slice(start, start + part), slice(quarter + start, quarter + start + part)
        signal_turns = quarter_turns([(phased[p, real, :LANES], phased[p, imag, :LANES]) for p in range(PHASES)])
        lag_turns = quarter_turns([(phased[p, real, LANES:], phased[p, imag, LANES:]) for p in range(PHASES)])
        through, lagged = [], []
        for (a_re, a_im), (b_re, b_im) in zip(signal_turns, lag_turns):
            b_im = jnp.where(low, b_im, -b_im)
            r_re, r_im = turned(a_re), turned(a_im)
            through.append((a_re * b_re - a_im * b_im, a_re * b_im + a_im * b_re))
            lagged.append((a_re * r_re + a_im * r_im, a_re * r_im - a_im * r_re))
        for cols, parts in ((slice(0, LANES), through), (slice(LANES, 2 * LANES), lagged)):
            turns = quarter_turns(parts)
            for phase in range(PHASES):
                value_re, value_im = turns[-phase % PHASES]
                spectra[phase, real, cols] = value_re.astype(jnp.bfloat16)
                spectra[phase, imag, cols] = value_im.astype(jnp.bfloat16)

    low = lower_lanes(quarter)
    for phase in range(PHASES):
        here = slice(phase * quarter, (phase + 1) * quarter)
        spread = pl.ds(phase, quarter, stride=PHASES)
        result = jnp.dot(back[phase], spectra[phase], preferred_element_type=jnp.float32)
        pair = wide(result[:, :LANES].astype(jnp.bfloat16))
        other = turned(pair)
        pairs[spread, :] = pair
        grad_q[spread, :] = turned(conv_qc[here, :]) * jnp.where(low, pair, other)
        grad_kv[spread, :] = jnp.where(low, other, pair) * turned(conv_kv[here, :])
        lag_grad[spread, :] = result[:, LANES:] * scale

    extra[...] = jnp.zeros_like(extra)
    tap_sum_kv = [jnp.zeros((EDGE, LANES), jnp.float32)] * tap_count
    tap_sum_q = [jnp.zeros((EDGE, LANES), jnp.float32)] * tap_count
    part = min(32, rows)
    for base in range(0, total, part):
        kv = grad_kv[base : base + part, :]
        q = grad_q[base : base + part, :]
        for j in range(tap_count):
            window = slice(base + EDGE - j, base + EDGE - j + part)
            tap_sum_kv[j] = tap_sum_kv[j] + jnp.sum((kv * raw_kv[window, :]).reshape(part // EDGE, EDGE, LANES), axis=0)
            tap_sum_q[j] = tap_sum_q[j] + jnp.sum((q * raw_qc[window, :]).reshape(part // EDGE, EDGE, LANES), axis=0)
    spare = [jnp.zeros((1, LANES), jnp.float32)] * (EDGE - tap_count)
    sums = [
        jnp.concatenate([jnp.sum(s, axis=0, keepdims=True) for s in parts] + spare, axis=0) * scale
        for parts in (tap_sum_kv, tap_sum_q)
    ]
    reach = tap_count - 1
    low_taps, low_reach = lower_lanes(tap_count), lower_lanes(reach)
    sums_kv, sums_q = [s[:tap_count] for s in sums]
    high_q = wide(sums_q.astype(jnp.bfloat16))
    extra[3 * reach : 3 * reach + tap_count, :] = sums_kv
    extra[3 * reach + tap_count : 3 * reach + 2 * tap_count, :] = jnp.where(low_taps, high_q, turned(sums_q - high_q))
    for step in range(count):
        owner = partner(me, back_offsets[step], 1, count)
        base = pl.multiple_of(owner * rows, rows)
        out = out_refs[step]
        out[0:rows, :] = pairs[pl.ds(base, rows), :].astype(jnp.bfloat16)
        out[rows : rows + half_rows, :] = jnp.where(
            low_half, lag_grad[pl.ds(base, half_rows), :], turned(lag_grad[pl.ds(base + half_rows, half_rows), :])
        ).astype(jnp.bfloat16)
        extra[0:reach, :] = raw_kv[pl.ds(base + EDGE - reach, reach), :]
        extra[reach : 2 * reach, :] = grad_kv[pl.ds(base + rows, reach), :]
        extra[2 * reach : 3 * reach, :] = jnp.where(
            low_reach, raw_qc[pl.ds(base + EDGE - reach, reach), :], turned(grad_q[pl.ds(base + rows, reach), :])
        )
        out[rows + half_rows :, :] = extra[: out.shape[0] - rows - half_rows, :].astype(jnp.bfloat16)


def shifted_sum(taps, padded, first, direction, rows):
    return sum(taps[j] * padded[first + direction * j : first + direction * j + rows, :] for j in range(len(taps)))


def local_kernel(tap_count, streams_hbm, taps_hbm, cotangent_hbm, high_hbm, rest_hbm, back_hbm, arrived_ref, *refs):
    conv_ref, taps_ref, cotangent_ref, high_ref, rest_ref, back_ref, streams_ref, padded, sems = refs
    pairs = (
        (streams_hbm, streams_ref), (taps_hbm, taps_ref), (cotangent_hbm, cotangent_ref),
        (high_hbm, high_ref), (rest_hbm, rest_ref), (back_hbm, back_ref),
    )
    copies = [pltpu.make_async_copy(here, there, sems.at[k]) for k, (here, there) in enumerate(pairs)]
    for copy in copies:
        copy.start()
    copies[0].wait()
    copies[1].wait()
    streams, rows, channels = conv_ref.shape
    padded[0:EDGE, :] = jnp.zeros((EDGE, LANES), jnp.float32)
    for i in range(streams):
        for start in range(0, channels, LANES):
            cols = slice(start, start + LANES)
            padded[EDGE:, :] = wide(streams_ref[i, :, cols])
            taps = [taps_ref[i, j : j + 1, cols] for j in range(tap_count)]
            conv_ref[i, :, cols] = shifted_sum(taps, padded, EDGE, -1, rows)
    for copy in copies[2:]:
        copy.wait()


def finish_kernel(count, tap_count, *refs):
    in_refs = refs[:count]
    conv_ref, taps_ref, cotangent_ref = refs[count : count + 3]
    out_hbm = refs[count + 3 : count + 7]
    gated_ref, stream_ref, lag_ref, tap_ref, blocks, extras, edges, grads, sems, tap_sem = refs[count + 7 :]
    me = lax.axis_index("ctx")
    offsets = step_offsets(count, back=True)
    rows = gated_ref.shape[0]
    half_rows = rows // 2
    reach = tap_count - 1
    low = lower_lanes(rows)
    low_half = lower_lanes(half_rows)
    extent = extras.shape[1] - EDGE
    low_extra = lower_lanes(extent)
    low_taps = lower_lanes(tap_count)
    for step in range(count):
        owner = partner(me, offsets[step], -1, count)
        blocks[owner, :, :] = in_refs[step][...]
    edges[...] = jnp.zeros_like(edges)
    copies = []
    for pair in range(count // 2):
        cols = slice(pair * LANES, (pair + 1) * LANES)

        def both(window, mask):
            even, odd = wide(blocks[2 * pair, window, :]), wide(blocks[2 * pair + 1, window, :])
            return jnp.where(mask, even, turned(odd)), jnp.where(mask, turned(even), odd)

        extra_rows = slice(rows + half_rows, None)
        extras[0, :extent, :], extras[1, :extent, :] = both(extra_rows, low_extra)
        mixed, product_grad = both(slice(0, rows), low)
        lag_lower, lag_upper = both(slice(rows, rows + half_rows), low_half)
        lag_ref[0:half_rows, cols] = lag_lower.astype(jnp.bfloat16)
        lag_ref[half_rows:, cols] = lag_upper.astype(jnp.bfloat16)
        taps = [[taps_ref[i, j : j + 1, cols] for j in range(tap_count)] for i in range(3)]
        befores = (extras[0, 2 * reach : 3 * reach, :], extras[0, 0:reach, :], extras[1, 0:reach, :])
        afters = (extras[1, 2 * reach : 3 * reach, :], extras[0, reach : 2 * reach, :], extras[1, reach : 2 * reach, :])
        convolved = []
        for i in range(3):
            edges[i, EDGE - reach : EDGE, :] = befores[i]
            first = conv_ref[i, 0:EDGE, cols] + shifted_sum(taps[i], edges.at[i], EDGE, -1, EDGE)
            convolved.append(jnp.concatenate([first, conv_ref[i, EDGE:, cols]], axis=0))
        query, key, value = convolved
        gated_ref[:, cols] = (query * mixed).astype(jnp.bfloat16)
        own = (wide(cotangent_ref[:, cols]) * mixed, product_grad * value, product_grad * key)
        for i in range(3):
            grads[i, 0:rows, :] = own[i]
            grads[i, rows : rows + reach, :] = afters[i]
            stream_ref[i, :, cols] = shifted_sum(taps[i], grads.at[i], 0, 1, rows).astype(jnp.bfloat16)
        sums_kv = slice(3 * reach, 3 * reach + tap_count)
        sums_q = slice(3 * reach + tap_count, 3 * reach + 2 * tap_count)
        tap_ref[1, :, cols] = extras[0, sums_kv, :]
        tap_ref[2, :, cols] = extras[1, sums_kv, :]
        tap_ref[0, :, cols] = extras[0, sums_q, :] + extras[1, sums_q, :]
        held = (gated_ref.at[:, cols], stream_ref.at[:, :, cols], lag_ref.at[:, cols])
        there = (out_hbm[0].at[:, cols], out_hbm[1].at[:, :, cols], out_hbm[2].at[:, cols])
        for k in range(3):
            copies.append(pltpu.make_async_copy(held[k], there[k], sems.at[pair, k]))
            copies[-1].start()
    copies.append(pltpu.make_async_copy(tap_ref, out_hbm[3], tap_sem.at[0]))
    copies[-1].start()
    for copy in copies:
        copy.wait()


def exchanged(blocks, back=False):
    count = len(blocks)
    return [blocks[0]] + [
        lax.ppermute(block, "ctx", [(source, partner(source, offset, 1, count)) for source in range(count)])
        for block, offset in zip(blocks[1:], step_offsets(count, back)[1:])
    ]


def in_hbm(array):
    return pltpu.with_memory_space_constraint(array, pltpu.HBM)


def in_vmem(count):
    return [pl.BlockSpec(memory_space=pltpu.VMEM)] * count


def local_dense(streams, taps, filters, cotangent):
    count = lax.axis_size("ctx")
    rows, channels = filters.shape
    tap_count = taps.shape[1]
    total = rows * count
    params = pltpu.CompilerParams(vmem_limit_bytes=VMEM_BYTES)
    sent_rows = 2 * rows + rows // 2
    packed = pl.pallas_call(
        functools.partial(pack_kernel, count),
        out_shape=[jax.ShapeDtypeStruct((sent_rows, LANES), jnp.bfloat16)] * count
        + [jax.ShapeDtypeStruct((2 * EDGE, LANES), jnp.float32)],
        in_specs=[pl.BlockSpec(memory_space=pltpu.HBM)] * 4,
        out_specs=in_vmem(count + 1),
        scratch_shapes=[pltpu.VMEM(a.shape, a.dtype) for a in (streams, filters, cotangent, taps)]
        + [pltpu.SemaphoreType.DMA((5,))],
        compiler_params=params,
        name="pack",
    )(*[in_hbm(a) for a in (streams, filters, cotangent, taps)])
    arrived = exchanged(packed[:count])
    quarter = total // PHASES
    tables = phase_tables(total)
    hbm = pl.BlockSpec(memory_space=pltpu.HBM)
    conv, taps_here, cotangent_here, *tables_here = pl.pallas_call(
        functools.partial(local_kernel, tap_count),
        out_shape=[
            jax.ShapeDtypeStruct(streams.shape, jnp.float32),
            jax.ShapeDtypeStruct(taps.shape, taps.dtype),
            jax.ShapeDtypeStruct(cotangent.shape, cotangent.dtype),
            *[jax.ShapeDtypeStruct(table.shape, jnp.bfloat16) for table in tables],
        ],
        in_specs=[hbm] * (3 + len(tables)) + [pl.BlockSpec(memory_space=pl.ANY)],
        out_specs=in_vmem(3 + len(tables)),
        scratch_shapes=[
            pltpu.VMEM(streams.shape, streams.dtype),
            pltpu.VMEM((rows + EDGE, LANES), jnp.float32),
            pltpu.SemaphoreType.DMA((3 + len(tables),)),
        ],
        compiler_params=params,
        name="local",
    )(*[in_hbm(jnp.asarray(a)) for a in (streams, taps, cotangent, *tables)], arrived[min(2, count - 1)])
    extra_rows = -(-(5 * tap_count - 3) // ROW_TILE) * ROW_TILE
    back_rows = rows + rows // 2 + extra_rows
    f32_rows = lambda extent: pltpu.VMEM((extent, LANES), jnp.float32)
    made = pl.pallas_call(
        functools.partial(main_kernel, count, tap_count, 1.0 / math.sqrt(total)),
        out_shape=[jax.ShapeDtypeStruct((back_rows, LANES), jnp.bfloat16)] * count,
        in_specs=in_vmem(count + 1 + len(tables)),
        out_specs=in_vmem(count),
        scratch_shapes=[
            f32_rows(total + 2 * EDGE), f32_rows(total + 2 * EDGE), f32_rows(total + EDGE), f32_rows(total), f32_rows(total),
            pltpu.VMEM((total, 2 * LANES), jnp.bfloat16),
            pltpu.VMEM((PHASES, 2 * quarter, 2 * LANES), jnp.float32),
            pltpu.VMEM((PHASES, 2 * quarter, 2 * LANES), jnp.bfloat16),
            f32_rows(total + EDGE), f32_rows(total + EDGE), f32_rows(total + EDGE), f32_rows(total + EDGE),
            f32_rows(extra_rows + EDGE),
        ],
        compiler_params=params,
        name="channels",
    )(*arrived, packed[count], *tables_here)
    returned = exchanged(made, back=True)
    outs = [
        jax.ShapeDtypeStruct(filters.shape, jnp.bfloat16),
        jax.ShapeDtypeStruct(streams.shape, jnp.bfloat16),
        jax.ShapeDtypeStruct(filters.shape, jnp.bfloat16),
        jax.ShapeDtypeStruct(taps.shape, jnp.float32),
    ]
    return tuple(
        pl.pallas_call(
            functools.partial(finish_kernel, count, tap_count),
            out_shape=outs,
            in_specs=in_vmem(count + 3),
            out_specs=[hbm] * len(outs),
            scratch_shapes=[pltpu.VMEM(out.shape, out.dtype) for out in outs]
            + [
                pltpu.VMEM((count, back_rows, LANES), jnp.bfloat16),
                pltpu.VMEM((2, extra_rows + EDGE, LANES), jnp.float32),
                pltpu.VMEM((3, 2 * EDGE, LANES), jnp.float32),
                pltpu.VMEM((3, rows + 2 * EDGE, LANES), jnp.float32),
                pltpu.SemaphoreType.DMA((count // 2, 3)),
                pltpu.SemaphoreType.DMA((1,)),
            ],
            compiler_params=params,
            name="finish",
        )(*returned, conv, taps_here, cotangent_here)
    )


def shifted(value, axis, steps):
    count = lax.axis_size(axis)
    first, last = (max(0, -steps), min(count, count - steps))
    return lax.ppermute(value, axis, [(source, source + steps) for source in range(first, last)])


def angle_table(row_count, col_count, col_start, period):
    row_ids = lax.iota(jnp.int32, row_count)
    col_ids = col_start + lax.iota(jnp.int32, col_count)
    turns = row_ids[:, None] * col_ids[None, :] % period
    angles = turns.astype(jnp.float32) * (2.0 * math.pi / period)
    return (jnp.cos(angles), jnp.sin(angles))


def column_start():
    return 0


def split_product(table, signal):
    high_part = table.astype(jnp.bfloat16)
    low_part = (table - high_part.astype(jnp.float32)).astype(jnp.bfloat16)
    first = jnp.einsum("kt,ctu->cku", high_part, signal, preferred_element_type=jnp.float32)
    second = jnp.einsum("kt,ctu->cku", low_part, signal, preferred_element_type=jnp.float32)
    return first + second


def forward_transform(signal):
    input_rows = signal.shape[1]
    row_count = 2 * input_rows
    col_count = signal.shape[2]
    period = row_count * col_count
    cos_first, sin_first = angle_table(row_count, input_rows, 0, row_count)
    first_re = split_product(cos_first, signal)
    first_im = -split_product(sin_first, signal)
    cos_twist, sin_twist = angle_table(row_count, col_count, column_start(), period)
    turned_re = first_re * cos_twist + first_im * sin_twist
    turned_im = first_im * cos_twist - first_re * sin_twist
    cos_second, sin_second = angle_table(col_count, col_count, 0, col_count)
    spec_re = jnp.einsum("cut,tk->cuk", turned_re, cos_second, precision=exact_mode) + jnp.einsum(
        "cut,tk->cuk", turned_im, sin_second, precision=exact_mode
    )
    spec_im = jnp.einsum("cut,tk->cuk", turned_im, cos_second, precision=exact_mode) - jnp.einsum(
        "cut,tk->cuk", turned_re, sin_second, precision=exact_mode
    )
    return (spec_re, spec_im)


def inverse_transform(spec_re, spec_im, keep_rows):
    full_width = spec_re.shape[2]
    cos_second, sin_second = angle_table(full_width, full_width, 0, full_width)
    back_re = jnp.einsum("cuk,kt->cut", spec_re, cos_second, precision=exact_mode) - jnp.einsum(
        "cuk,kt->cut", spec_im, sin_second, precision=exact_mode
    )
    back_im = jnp.einsum("cuk,kt->cut", spec_im, cos_second, precision=exact_mode) + jnp.einsum(
        "cuk,kt->cut", spec_re, sin_second, precision=exact_mode
    )
    row_count = back_re.shape[1]
    col_count = back_re.shape[2]
    period = row_count * full_width
    cos_twist, sin_twist = angle_table(row_count, col_count, column_start(), period)
    turned_re = back_re * cos_twist - back_im * sin_twist
    turned_im = back_im * cos_twist + back_re * sin_twist
    cos_first, sin_first = angle_table(keep_rows, row_count, 0, row_count)
    result = jnp.einsum("tk,cku->ctu", cos_first, turned_re, precision=exact_mode) - jnp.einsum(
        "tk,cku->ctu", sin_first, turned_im, precision=exact_mode
    )
    return result * (1.0 / period)


def regroup_out(stacked):
    count_here = stacked.shape[0]
    channel_count = stacked.shape[1]
    block_rows = stacked.shape[2]
    shaped = stacked.reshape(count_here, channel_count, 1, block_rows)
    return lax.all_to_all(shaped, "ctx", split_axis=1, concat_axis=2, tiled=True)


def regroup_back(stacked):
    count_here = stacked.shape[0]
    arrived = lax.all_to_all(stacked, "ctx", split_axis=2, concat_axis=1, tiled=True)
    return arrived.reshape(count_here, arrived.shape[1], arrived.shape[3])


def merged(block):
    return block.reshape(block.shape[0] * block.shape[1], block.shape[2], block.shape[3])


def local_factored(streams, taps, filters, cotangent):
    block_rows = streams.shape[1]
    tap_reach = taps.shape[1] - 1
    earlier = shifted(streams[:, block_rows - tap_reach :, :], "ctx", 1)
    extended = jnp.concatenate([earlier, streams], axis=1).astype(jnp.float32)
    convolved = jnp.zeros((3, block_rows, streams.shape[2]), jnp.float32)
    for offset in range(tap_reach + 1):
        convolved = (
            convolved
            + taps[:, offset, None, :]
            * extended[:, tap_reach - offset : tap_reach - offset + block_rows, :]
        )
    query_side = convolved[0]
    key_side = convolved[1]
    value_side = convolved[2]
    product = (key_side * value_side).astype(jnp.bfloat16)
    seq_total = block_rows * lax.axis_size("ctx")
    scale_factor = 1.0 / math.sqrt(seq_total)
    arrived = regroup_out(jnp.stack([product, filters]).swapaxes(1, 2))
    per_stream = arrived.shape[1]
    grid_rows = arrived.shape[2]
    first_re, first_im = forward_transform(merged(arrived))
    prod_re = first_re[:per_stream]
    prod_im = first_im[:per_stream]
    filt_re = first_re[per_stream:]
    filt_im = first_im[per_stream:]
    mixed_re = prod_re * filt_re - prod_im * filt_im
    mixed_im = prod_re * filt_im + prod_im * filt_re
    mixed_cols = inverse_transform(mixed_re, mixed_im, grid_rows).astype(jnp.bfloat16)
    mixed_back = regroup_back(mixed_cols.reshape(1, per_stream, grid_rows, mixed_cols.shape[2]))
    mixed = mixed_back[0].T.astype(jnp.float32)
    gated = (query_side * mixed).astype(jnp.bfloat16)
    upstream = cotangent.astype(jnp.float32)
    mixed_grad = (upstream * query_side).astype(jnp.bfloat16)
    query_grad = upstream * mixed
    grad_cols = regroup_out(mixed_grad.T[None])
    grad_re, grad_im = forward_transform(merged(grad_cols))
    through_re = filt_re * grad_re + filt_im * grad_im
    through_im = filt_re * grad_im - filt_im * grad_re
    lagged_re = prod_re * grad_re + prod_im * grad_im
    lagged_im = prod_re * grad_im - prod_im * grad_re
    both_times = inverse_transform(
        jnp.concatenate([through_re, lagged_re], axis=0),
        jnp.concatenate([through_im, lagged_im], axis=0),
        grid_rows,
    )
    product_grad_cols = both_times[:per_stream].astype(jnp.bfloat16)
    filter_grad_cols = (both_times[per_stream:] * scale_factor).astype(jnp.bfloat16)
    returned = regroup_back(jnp.stack([product_grad_cols, filter_grad_cols]))
    product_grad = returned[0].T.astype(jnp.float32)
    filter_grad = returned[1].T
    conv_grad = jnp.stack([query_grad, product_grad * value_side, product_grad * key_side])
    following = shifted(conv_grad[:, :tap_reach, :].astype(jnp.bfloat16), "ctx", -1).astype(
        jnp.float32
    )
    extended_grad = jnp.concatenate([conv_grad, following], axis=1)
    running = jnp.zeros((3, block_rows, streams.shape[2]), jnp.float32)
    for offset in range(tap_reach + 1):
        running = (
            running + taps[:, offset, None, :] * extended_grad[:, offset : offset + block_rows, :]
        )
    stream_grad = running.astype(jnp.bfloat16)
    tap_terms = jnp.stack(
        [
            jnp.sum(
                conv_grad * extended[:, tap_reach - offset : tap_reach - offset + block_rows, :],
                axis=1,
            )
            for offset in range(tap_reach + 1)
        ],
        axis=1,
    )
    tap_grad = lax.psum(tap_terms, "ctx") * scale_factor
    return (gated, stream_grad, filter_grad, tap_grad)


def local(streams, taps, filters, cotangent):
    count = lax.axis_size("ctx")
    rows, channels = filters.shape
    tap_count = taps.shape[1]
    pairs_fill_lanes = channels == count * HALF and count % 2 == 0
    short_enough = rows % LANES == 0 and 3 * (rows * count) ** 2 <= TABLE_BYTES and tap_count < EDGE
    if pairs_fill_lanes and short_enough:
        return local_dense(streams, taps, filters, cotangent)
    return local_factored(streams, taps, filters, cotangent)


def solution(mesh):
    in_specs = (P(None, "ctx", "fft"), P(None, None, "fft"), P("ctx", "fft"), P("ctx", "fft"))
    out_specs = (P("ctx", "fft"), P(None, "ctx", "fft"), P("ctx", "fft"), P(None, None, "fft"))
    return jax.shard_map(local, mesh=mesh, in_specs=in_specs, out_specs=out_specs, check_vma=False)
```

```python
import functools
import math

import jax
import jax.numpy as jnp
import numpy as np
from jax import lax
from jax.experimental import pallas as pl
from jax.experimental.pallas import tpu as pltpu
from jax.sharding import PartitionSpec as P

exact_mode = lax.Precision.HIGHEST
LANES = 128
HALF = LANES // 2
PHASES = 4
EDGE = 8
ROW_TILE = 16
TABLE_BYTES = 16 * 1024 * 1024
VMEM_BYTES = 32 * 1024 * 1024


def step_offsets(count, back=False):
    groups = count // 2
    far = groups // 2
    near = [g for g in range(1, groups) if g != far]
    first, last = near[:1], near[1:]
    if back:
        order = [(far, 0)] + [(g, m) for g in first for m in (0, 1)] + [(far, 1)]
        order = order + [(g, 1) for g in last] + [(g, 0) for g in last] + [(0, 1)]
    else:
        order = [(far, 0), (0, 1), (far, 1)] + [(g, m) for g in first for m in (1, 0)]
        order = order + [(g, 1) for g in last] + [(g, 0) for g in last]
    return [(0, 0)] + [offset for offset in dict.fromkeys(order) if offset != (0, 0)]


def partner(index, offset, sign, count):
    group, member = offset
    groups = count // 2
    moved = (index // 2 + sign * group + groups) % groups
    flipped = (index + member) % 2
    return moved * 2 + flipped


def lower_lanes(rows):
    return lax.broadcasted_iota(jnp.int32, (rows, LANES), 1) < HALF


def turned(value):
    return pltpu.roll(value, HALF, 1)


def wide(value):
    return value.astype(jnp.float32)


def paired(first, second, odd, low):
    left = pltpu.roll(first, odd * HALF, 1)
    right = pltpu.roll(second, HALF - odd * HALF, 1)
    return jnp.where(low, left, right).astype(jnp.bfloat16)


def pack_kernel(count, *refs):
    streams_hbm, filters_hbm, cotangent_hbm, taps_hbm = refs[:4]
    out_refs = refs[4 : 5 + count]
    streams_ref, filters_ref, cotangent_ref, taps_ref, sems = refs[5 + count :]
    me = lax.axis_index("ctx")
    offsets = step_offsets(count)
    rows = filters_ref.shape[0]
    half_rows = rows // 2
    tap_count = taps_ref.shape[1]
    low = lower_lanes(rows)
    low_half = lower_lanes(half_rows)
    moves = (
        (filters_hbm, filters_ref), (streams_hbm.at[1:], streams_ref.at[1:]), (streams_hbm.at[:1], streams_ref.at[:1]),
        (cotangent_hbm, cotangent_ref), (taps_hbm, taps_ref),
    )
    copies = [pltpu.make_async_copy(here, there, sems.at[k]) for k, (here, there) in enumerate(moves)]
    for copy in copies:
        copy.start()

    def place(owner):
        return pl.ds(pl.multiple_of(owner // 2 * LANES, LANES), LANES), lax.rem(owner, 2)

    places = [place(partner(me, offsets[step], 1, count)) for step in range(count)]
    copies[0].wait()
    for (cols, odd), out in zip(places, out_refs):
        lag_block = wide(filters_ref[:, cols])
        out[2 * rows :, :] = paired(lag_block[:half_rows], lag_block[half_rows:], odd, low_half)
    copies[1].wait()
    for (cols, odd), out in zip(places, out_refs):
        out[0:rows, :] = paired(wide(streams_ref[1, :, cols]), wide(streams_ref[2, :, cols]), odd, low)
    copies[2].wait()
    copies[3].wait()
    for (cols, odd), out in zip(places, out_refs):
        out[rows : 2 * rows, :] = paired(wide(streams_ref[0, :, cols]), wide(cotangent_ref[:, cols]), odd, low)
    copies[4].wait()
    cols, odd = place(me)
    tap_out = out_refs[count]
    low_taps = lower_lanes(tap_count)
    here = [pltpu.roll(taps_ref[i, :, cols], odd * HALF, 1) for i in range(3)]
    first_tap = lax.broadcasted_iota(jnp.int32, (tap_count, LANES), 0) == 0
    tap_out[...] = jnp.zeros_like(tap_out)
    tap_out[0:tap_count, :] = jnp.where(low_taps, here[1], turned(here[2]))
    tap_out[EDGE : EDGE + tap_count, :] = jnp.where(low_taps, here[0], jnp.where(first_tap, 1.0, 0.0))


def phase_tables(total):
    quarter = total // PHASES
    freq = 2 * np.arange(quarter)[:, None] + 1
    ahead, back = [], []
    for phase in range(PHASES):
        place = PHASES * np.arange(quarter)[None, :] + phase
        angles = (freq * place % (4 * total)) * (math.pi / (2 * total))
        table = np.concatenate([np.cos(angles), -np.sin(angles)])
        ahead.append(table)
        back.append(table.T / total)
    ahead = np.stack(ahead)
    high = ahead.astype(jnp.bfloat16)
    rest = (ahead - high.astype(np.float64)).astype(jnp.bfloat16)
    return high, rest, np.stack(back).astype(jnp.bfloat16)


def quarter_turns(parts):
    (r0, i0), (r1, i1), (r2, i2), (r3, i3) = parts
    even_r, even_i, odd_r, odd_i = r0 + r2, i0 + i2, r1 + r3, i1 + i3
    gap_r, gap_i, side_r, side_i = r0 - r2, i0 - i2, r1 - r3, i1 - i3
    return [
        (even_r + odd_r, even_i + odd_i),
        (gap_r - side_i, gap_i + side_r),
        (even_r - odd_r, even_i - odd_i),
        (gap_r + side_i, gap_i - side_r),
    ]


def main_kernel(count, tap_count, scale, *refs):
    in_refs = refs[:count]
    tap_ref, high, rest, back = refs[count : count + 4]
    out_refs = refs[count + 4 : 2 * count + 4]
    (raw_kv, raw_qc, raw_lag, conv_kv, conv_qc, signals, phased, spectra, pairs, grad_kv, grad_q, lag_grad, extra) = refs[
        2 * count + 4 :
    ]
    me = lax.axis_index("ctx")
    offsets, back_offsets = step_offsets(count), step_offsets(count, back=True)
    total = signals.shape[0]
    quarter = total // PHASES
    rows = total // count
    half_rows = rows // 2
    low_half = lower_lanes(half_rows)

    raw_kv[0:EDGE, :] = jnp.zeros((EDGE, LANES), jnp.float32)
    raw_qc[0:EDGE, :] = jnp.zeros((EDGE, LANES), jnp.float32)
    grad_kv[total:, :] = jnp.zeros((EDGE, LANES), jnp.float32)
    grad_q[total:, :] = jnp.zeros((EDGE, LANES), jnp.float32)
    for step in range(count):
        source = partner(me, offsets[step], -1, count)
        base = pl.multiple_of(source * rows, rows)
        block = in_refs[step]
        raw_kv[pl.ds(base + EDGE, rows), :] = wide(block[0:rows, :])
        raw_qc[pl.ds(base + EDGE, rows), :] = wide(block[rows : 2 * rows, :])
        lag_block = wide(block[2 * rows :, :])
        other = turned(lag_block)
        raw_lag[pl.ds(base, half_rows), :] = jnp.where(low_half, lag_block, other)
        raw_lag[pl.ds(base + half_rows, half_rows), :] = jnp.where(low_half, other, lag_block)

    tap_kv = [tap_ref[j : j + 1, :] for j in range(tap_count)]
    tap_q = [tap_ref[EDGE + j : EDGE + j + 1, :] for j in range(tap_count)]

    part = min(32, quarter)
    low = lower_lanes(part)
    for start in range(0, quarter, part):
        for phase in range(PHASES):
            first = PHASES * start + phase
            here = slice(phase * quarter + start, phase * quarter + start + part)
            key_value = jnp.zeros((part, LANES), jnp.float32)
            query_cot = jnp.zeros((part, LANES), jnp.float32)
            for j in range(tap_count):
                window = pl.ds(first + EDGE - j, part, stride=PHASES)
                key_value = key_value + tap_kv[j] * raw_kv[window, :]
                query_cot = query_cot + tap_q[j] * raw_qc[window, :]
            conv_kv[here, :] = key_value
            conv_qc[here, :] = query_cot
            product = key_value * turned(key_value)
            mixed_grad = query_cot * turned(query_cot)
            signals[here, :LANES] = jnp.where(low, product, mixed_grad).astype(jnp.bfloat16)
            signals[here, LANES:] = raw_lag[pl.ds(first, part, stride=PHASES), :].astype(jnp.bfloat16)

    for phase in range(PHASES):
        signal = signals[phase * quarter : (phase + 1) * quarter, :]
        phased[phase, :, :] = jnp.dot(high[phase], signal, preferred_element_type=jnp.float32) + jnp.dot(
            rest[phase], signal, preferred_element_type=jnp.float32
        )

    part = min(16, quarter)
    low = lower_lanes(part)
    for start in range(0, quarter, part):
        real, imag = slice(start, start + part), slice(quarter + start, quarter + start + part)
        signal_turns = quarter_turns([(phased[p, real, :LANES], phased[p, imag, :LANES]) for p in range(PHASES)])
        lag_turns = quarter_turns([(phased[p, real, LANES:], phased[p, imag, LANES:]) for p in range(PHASES)])
        through, lagged = [], []
        for (a_re, a_im), (b_re, b_im) in zip(signal_turns, lag_turns):
            b_im = jnp.where(low, b_im, -b_im)
            r_re, r_im = turned(a_re), turned(a_im)
            through.append((a_re * b_re - a_im * b_im, a_re * b_im + a_im * b_re))
            lagged.append((a_re * r_re + a_im * r_im, a_re * r_im - a_im * r_re))
        for cols, parts in ((slice(0, LANES), through), (slice(LANES, 2 * LANES), lagged)):
            turns = quarter_turns(parts)
            for phase in range(PHASES):
                value_re, value_im = turns[-phase % PHASES]
                spectra[phase, real, cols] = value_re.astype(jnp.bfloat16)
                spectra[phase, imag, cols] = value_im.astype(jnp.bfloat16)

    low = lower_lanes(quarter)
    for phase in range(PHASES):
        here = slice(phase * quarter, (phase + 1) * quarter)
        spread = pl.ds(phase, quarter, stride=PHASES)
        result = jnp.dot(back[phase], spectra[phase], preferred_element_type=jnp.float32)
        pair = wide(result[:, :LANES].astype(jnp.bfloat16))
        other = turned(pair)
        pairs[spread, :] = pair
        grad_q[spread, :] = turned(conv_qc[here, :]) * jnp.where(low, pair, other)
        grad_kv[spread, :] = jnp.where(low, other, pair) * turned(conv_kv[here, :])
        lag_grad[spread, :] = result[:, LANES:] * scale

    extra[...] = jnp.zeros_like(extra)
    tap_sum_kv = [jnp.zeros((EDGE, LANES), jnp.float32)] * tap_count
    tap_sum_q = [jnp.zeros((EDGE, LANES), jnp.float32)] * tap_count
    part = min(32, rows)
    for base in range(0, total, part):
        kv = grad_kv[base : base + part, :]
        q = grad_q[base : base + part, :]
        for j in range(tap_count):
            window = slice(base + EDGE - j, base + EDGE - j + part)
            tap_sum_kv[j] = tap_sum_kv[j] + jnp.sum((kv * raw_kv[window, :]).reshape(part // EDGE, EDGE, LANES), axis=0)
            tap_sum_q[j] = tap_sum_q[j] + jnp.sum((q * raw_qc[window, :]).reshape(part // EDGE, EDGE, LANES), axis=0)
    spare = [jnp.zeros((1, LANES), jnp.float32)] * (EDGE - tap_count)
    sums = [
        jnp.concatenate([jnp.sum(s, axis=0, keepdims=True) for s in parts] + spare, axis=0) * scale
        for parts in (tap_sum_kv, tap_sum_q)
    ]
    reach = tap_count - 1
    low_taps, low_reach = lower_lanes(tap_count), lower_lanes(reach)
    sums_kv, sums_q = [s[:tap_count] for s in sums]
    high_q = wide(sums_q.astype(jnp.bfloat16))
    extra[3 * reach : 3 * reach + tap_count, :] = sums_kv
    extra[3 * reach + tap_count : 3 * reach + 2 * tap_count, :] = jnp.where(low_taps, high_q, turned(sums_q - high_q))
    for step in range(count):
        owner = partner(me, back_offsets[step], 1, count)
        base = pl.multiple_of(owner * rows, rows)
        out = out_refs[step]
        out[0:rows, :] = pairs[pl.ds(base, rows), :].astype(jnp.bfloat16)
        out[rows : rows + half_rows, :] = jnp.where(
            low_half, lag_grad[pl.ds(base, half_rows), :], turned(lag_grad[pl.ds(base + half_rows, half_rows), :])
        ).astype(jnp.bfloat16)
        extra[0:reach, :] = raw_kv[pl.ds(base + EDGE - reach, reach), :]
        extra[reach : 2 * reach, :] = grad_kv[pl.ds(base + rows, reach), :]
        extra[2 * reach : 3 * reach, :] = jnp.where(
            low_reach, raw_qc[pl.ds(base + EDGE - reach, reach), :], turned(grad_q[pl.ds(base + rows, reach), :])
        )
        out[rows + half_rows :, :] = extra[: out.shape[0] - rows - half_rows, :].astype(jnp.bfloat16)


def shifted_sum(taps, padded, first, direction, rows):
    return sum(taps[j] * padded[first + direction * j : first + direction * j + rows, :] for j in range(len(taps)))


def local_kernel(tap_count, streams_hbm, taps_hbm, cotangent_hbm, high_hbm, rest_hbm, back_hbm, arrived_ref, *refs):
    conv_ref, taps_ref, cotangent_ref, high_ref, rest_ref, back_ref, streams_ref, padded, sems = refs
    pairs = (
        (streams_hbm, streams_ref), (taps_hbm, taps_ref), (cotangent_hbm, cotangent_ref),
        (high_hbm, high_ref), (rest_hbm, rest_ref), (back_hbm, back_ref),
    )
    copies = [pltpu.make_async_copy(here, there, sems.at[k]) for k, (here, there) in enumerate(pairs)]
    for copy in copies:
        copy.start()
    copies[0].wait()
    copies[1].wait()
    streams, rows, channels = conv_ref.shape
    padded[0:EDGE, :] = jnp.zeros((EDGE, LANES), jnp.float32)
    for i in range(streams):
        for start in range(0, channels, LANES):
            cols = slice(start, start + LANES)
            padded[EDGE:, :] = wide(streams_ref[i, :, cols])
            taps = [taps_ref[i, j : j + 1, cols] for j in range(tap_count)]
            conv_ref[i, :, cols] = shifted_sum(taps, padded, EDGE, -1, rows)
    for copy in copies[2:]:
        copy.wait()


def finish_kernel(count, tap_count, *refs):
    in_refs = refs[:count]
    conv_ref, taps_ref, cotangent_ref = refs[count : count + 3]
    out_hbm = refs[count + 3 : count + 7]
    gated_ref, stream_ref, lag_ref, tap_ref, blocks, extras, edges, grads, sems, tap_sem = refs[count + 7 :]
    me = lax.axis_index("ctx")
    offsets = step_offsets(count, back=True)
    rows = gated_ref.shape[0]
    half_rows = rows // 2
    reach = tap_count - 1
    low = lower_lanes(rows)
    low_half = lower_lanes(half_rows)
    extent = extras.shape[1] - EDGE
    low_extra = lower_lanes(extent)
    low_taps = lower_lanes(tap_count)
    for step in range(count):
        owner = partner(me, offsets[step], -1, count)
        blocks[owner, :, :] = in_refs[step][...]
    edges[...] = jnp.zeros_like(edges)
    copies = []
    for pair in range(count // 2):
        cols = slice(pair * LANES, (pair + 1) * LANES)

        def both(window, mask):
            even, odd = wide(blocks[2 * pair, window, :]), wide(blocks[2 * pair + 1, window, :])
            return jnp.where(mask, even, turned(odd)), jnp.where(mask, turned(even), odd)

        extra_rows = slice(rows + half_rows, None)
        extras[0, :extent, :], extras[1, :extent, :] = both(extra_rows, low_extra)
        mixed, product_grad = both(slice(0, rows), low)
        lag_lower, lag_upper = both(slice(rows, rows + half_rows), low_half)
        lag_ref[0:half_rows, cols] = lag_lower.astype(jnp.bfloat16)
        lag_ref[half_rows:, cols] = lag_upper.astype(jnp.bfloat16)
        taps = [[taps_ref[i, j : j + 1, cols] for j in range(tap_count)] for i in range(3)]
        befores = (extras[0, 2 * reach : 3 * reach, :], extras[0, 0:reach, :], extras[1, 0:reach, :])
        afters = (extras[1, 2 * reach : 3 * reach, :], extras[0, reach : 2 * reach, :], extras[1, reach : 2 * reach, :])
        convolved = []
        for i in range(3):
            edges[i, EDGE - reach : EDGE, :] = befores[i]
            first = conv_ref[i, 0:EDGE, cols] + shifted_sum(taps[i], edges.at[i], EDGE, -1, EDGE)
            convolved.append(jnp.concatenate([first, conv_ref[i, EDGE:, cols]], axis=0))
        query, key, value = convolved
        gated_ref[:, cols] = (query * mixed).astype(jnp.bfloat16)
        for k, held in ((0, gated_ref), (2, lag_ref)):
            copies.append(pltpu.make_async_copy(held.at[:, cols], out_hbm[k].at[:, cols], sems.at[pair, k]))
            copies[-1].start()
        own = (wide(cotangent_ref[:, cols]) * mixed, product_grad * value, product_grad * key)
        for i in range(3):
            grads[i, 0:rows, :] = own[i]
            grads[i, rows : rows + reach, :] = afters[i]
            stream_ref[i, :, cols] = shifted_sum(taps[i], grads.at[i], 0, 1, rows).astype(jnp.bfloat16)
        sums_kv = slice(3 * reach, 3 * reach + tap_count)
        sums_q = slice(3 * reach + tap_count, 3 * reach + 2 * tap_count)
        tap_ref[1, :, cols] = extras[0, sums_kv, :]
        tap_ref[2, :, cols] = extras[1, sums_kv, :]
        tap_ref[0, :, cols] = extras[0, sums_q, :] + extras[1, sums_q, :]
        copies.append(pltpu.make_async_copy(stream_ref.at[:, :, cols], out_hbm[1].at[:, :, cols], sems.at[pair, 1]))
        copies[-1].start()
    copies.append(pltpu.make_async_copy(tap_ref, out_hbm[3], tap_sem.at[0]))
    copies[-1].start()
    for copy in copies:
        copy.wait()


def exchanged(blocks, back=False):
    count = len(blocks)
    return [blocks[0]] + [
        lax.ppermute(block, "ctx", [(source, partner(source, offset, 1, count)) for source in range(count)])
        for block, offset in zip(blocks[1:], step_offsets(count, back)[1:])
    ]


def in_hbm(array):
    return pltpu.with_memory_space_constraint(array, pltpu.HBM)


def in_vmem(count):
    return [pl.BlockSpec(memory_space=pltpu.VMEM)] * count


def local_dense(streams, taps, filters, cotangent):
    count = lax.axis_size("ctx")
    rows, channels = filters.shape
    tap_count = taps.shape[1]
    total = rows * count
    params = pltpu.CompilerParams(vmem_limit_bytes=VMEM_BYTES)
    sent_rows = 2 * rows + rows // 2
    packed = pl.pallas_call(
        functools.partial(pack_kernel, count),
        out_shape=[jax.ShapeDtypeStruct((sent_rows, LANES), jnp.bfloat16)] * count
        + [jax.ShapeDtypeStruct((2 * EDGE, LANES), jnp.float32)],
        in_specs=[pl.BlockSpec(memory_space=pltpu.HBM)] * 4,
        out_specs=in_vmem(count + 1),
        scratch_shapes=[pltpu.VMEM(a.shape, a.dtype) for a in (streams, filters, cotangent, taps)]
        + [pltpu.SemaphoreType.DMA((5,))],
        compiler_params=params,
        name="pack",
    )(*[in_hbm(a) for a in (streams, filters, cotangent, taps)])
    arrived = exchanged(packed[:count])
    quarter = total // PHASES
    tables = phase_tables(total)
    hbm = pl.BlockSpec(memory_space=pltpu.HBM)
    conv, taps_here, cotangent_here, *tables_here = pl.pallas_call(
        functools.partial(local_kernel, tap_count),
        out_shape=[
            jax.ShapeDtypeStruct(streams.shape, jnp.float32),
            jax.ShapeDtypeStruct(taps.shape, taps.dtype),
            jax.ShapeDtypeStruct(cotangent.shape, cotangent.dtype),
            *[jax.ShapeDtypeStruct(table.shape, jnp.bfloat16) for table in tables],
        ],
        in_specs=[hbm] * (3 + len(tables)) + [pl.BlockSpec(memory_space=pl.ANY)],
        out_specs=in_vmem(3 + len(tables)),
        scratch_shapes=[
            pltpu.VMEM(streams.shape, streams.dtype),
            pltpu.VMEM((rows + EDGE, LANES), jnp.float32),
            pltpu.SemaphoreType.DMA((3 + len(tables),)),
        ],
        compiler_params=params,
        name="local",
    )(*[in_hbm(jnp.asarray(a)) for a in (streams, taps, cotangent, *tables)], arrived[min(2, count - 1)])
    extra_rows = -(-(5 * tap_count - 3) // ROW_TILE) * ROW_TILE
    back_rows = rows + rows // 2 + extra_rows
    f32_rows = lambda extent: pltpu.VMEM((extent, LANES), jnp.float32)
    made = pl.pallas_call(
        functools.partial(main_kernel, count, tap_count, 1.0 / math.sqrt(total)),
        out_shape=[jax.ShapeDtypeStruct((back_rows, LANES), jnp.bfloat16)] * count,
        in_specs=in_vmem(count + 1 + len(tables)),
        out_specs=in_vmem(count),
        scratch_shapes=[
            f32_rows(total + 2 * EDGE), f32_rows(total + 2 * EDGE), f32_rows(total + EDGE), f32_rows(total), f32_rows(total),
            pltpu.VMEM((total, 2 * LANES), jnp.bfloat16),
            pltpu.VMEM((PHASES, 2 * quarter, 2 * LANES), jnp.float32),
            pltpu.VMEM((PHASES, 2 * quarter, 2 * LANES), jnp.bfloat16),
            f32_rows(total + EDGE), f32_rows(total + EDGE), f32_rows(total + EDGE), f32_rows(total + EDGE),
            f32_rows(extra_rows + EDGE),
        ],
        compiler_params=params,
        name="channels",
    )(*arrived, packed[count], *tables_here)
    returned = exchanged(made, back=True)
    outs = [
        jax.ShapeDtypeStruct(filters.shape, jnp.bfloat16),
        jax.ShapeDtypeStruct(streams.shape, jnp.bfloat16),
        jax.ShapeDtypeStruct(filters.shape, jnp.bfloat16),
        jax.ShapeDtypeStruct(taps.shape, jnp.float32),
    ]
    return tuple(
        pl.pallas_call(
            functools.partial(finish_kernel, count, tap_count),
            out_shape=outs,
            in_specs=in_vmem(count + 3),
            out_specs=[hbm] * len(outs),
            scratch_shapes=[pltpu.VMEM(out.shape, out.dtype) for out in outs]
            + [
                pltpu.VMEM((count, back_rows, LANES), jnp.bfloat16),
                pltpu.VMEM((2, extra_rows + EDGE, LANES), jnp.float32),
                pltpu.VMEM((3, 2 * EDGE, LANES), jnp.float32),
                pltpu.VMEM((3, rows + 2 * EDGE, LANES), jnp.float32),
                pltpu.SemaphoreType.DMA((count // 2, 3)),
                pltpu.SemaphoreType.DMA((1,)),
            ],
            compiler_params=params,
            name="finish",
        )(*returned, conv, taps_here, cotangent_here)
    )


def shifted(value, axis, steps):
    count = lax.axis_size(axis)
    first, last = (max(0, -steps), min(count, count - steps))
    return lax.ppermute(value, axis, [(source, source + steps) for source in range(first, last)])


def angle_table(row_count, col_count, col_start, period):
    row_ids = lax.iota(jnp.int32, row_count)
    col_ids = col_start + lax.iota(jnp.int32, col_count)
    turns = row_ids[:, None] * col_ids[None, :] % period
    angles = turns.astype(jnp.float32) * (2.0 * math.pi / period)
    return (jnp.cos(angles), jnp.sin(angles))


def column_start():
    return 0


def split_product(table, signal):
    high_part = table.astype(jnp.bfloat16)
    low_part = (table - high_part.astype(jnp.float32)).astype(jnp.bfloat16)
    first = jnp.einsum("kt,ctu->cku", high_part, signal, preferred_element_type=jnp.float32)
    second = jnp.einsum("kt,ctu->cku", low_part, signal, preferred_element_type=jnp.float32)
    return first + second


def forward_transform(signal):
    input_rows = signal.shape[1]
    row_count = 2 * input_rows
    col_count = signal.shape[2]
    period = row_count * col_count
    cos_first, sin_first = angle_table(row_count, input_rows, 0, row_count)
    first_re = split_product(cos_first, signal)
    first_im = -split_product(sin_first, signal)
    cos_twist, sin_twist = angle_table(row_count, col_count, column_start(), period)
    turned_re = first_re * cos_twist + first_im * sin_twist
    turned_im = first_im * cos_twist - first_re * sin_twist
    cos_second, sin_second = angle_table(col_count, col_count, 0, col_count)
    spec_re = jnp.einsum("cut,tk->cuk", turned_re, cos_second, precision=exact_mode) + jnp.einsum(
        "cut,tk->cuk", turned_im, sin_second, precision=exact_mode
    )
    spec_im = jnp.einsum("cut,tk->cuk", turned_im, cos_second, precision=exact_mode) - jnp.einsum(
        "cut,tk->cuk", turned_re, sin_second, precision=exact_mode
    )
    return (spec_re, spec_im)


def inverse_transform(spec_re, spec_im, keep_rows):
    full_width = spec_re.shape[2]
    cos_second, sin_second = angle_table(full_width, full_width, 0, full_width)
    back_re = jnp.einsum("cuk,kt->cut", spec_re, cos_second, precision=exact_mode) - jnp.einsum(
        "cuk,kt->cut", spec_im, sin_second, precision=exact_mode
    )
    back_im = jnp.einsum("cuk,kt->cut", spec_im, cos_second, precision=exact_mode) + jnp.einsum(
        "cuk,kt->cut", spec_re, sin_second, precision=exact_mode
    )
    row_count = back_re.shape[1]
    col_count = back_re.shape[2]
    period = row_count * full_width
    cos_twist, sin_twist = angle_table(row_count, col_count, column_start(), period)
    turned_re = back_re * cos_twist - back_im * sin_twist
    turned_im = back_im * cos_twist + back_re * sin_twist
    cos_first, sin_first = angle_table(keep_rows, row_count, 0, row_count)
    result = jnp.einsum("tk,cku->ctu", cos_first, turned_re, precision=exact_mode) - jnp.einsum(
        "tk,cku->ctu", sin_first, turned_im, precision=exact_mode
    )
    return result * (1.0 / period)


def regroup_out(stacked):
    count_here = stacked.shape[0]
    channel_count = stacked.shape[1]
    block_rows = stacked.shape[2]
    shaped = stacked.reshape(count_here, channel_count, 1, block_rows)
    return lax.all_to_all(shaped, "ctx", split_axis=1, concat_axis=2, tiled=True)


def regroup_back(stacked):
    count_here = stacked.shape[0]
    arrived = lax.all_to_all(stacked, "ctx", split_axis=2, concat_axis=1, tiled=True)
    return arrived.reshape(count_here, arrived.shape[1], arrived.shape[3])


def merged(block):
    return block.reshape(block.shape[0] * block.shape[1], block.shape[2], block.shape[3])


def local_factored(streams, taps, filters, cotangent):
    block_rows = streams.shape[1]
    tap_reach = taps.shape[1] - 1
    earlier = shifted(streams[:, block_rows - tap_reach :, :], "ctx", 1)
    extended = jnp.concatenate([earlier, streams], axis=1).astype(jnp.float32)
    convolved = jnp.zeros((3, block_rows, streams.shape[2]), jnp.float32)
    for offset in range(tap_reach + 1):
        convolved = (
            convolved
            + taps[:, offset, None, :]
            * extended[:, tap_reach - offset : tap_reach - offset + block_rows, :]
        )
    query_side = convolved[0]
    key_side = convolved[1]
    value_side = convolved[2]
    product = (key_side * value_side).astype(jnp.bfloat16)
    seq_total = block_rows * lax.axis_size("ctx")
    scale_factor = 1.0 / math.sqrt(seq_total)
    arrived = regroup_out(jnp.stack([product, filters]).swapaxes(1, 2))
    per_stream = arrived.shape[1]
    grid_rows = arrived.shape[2]
    first_re, first_im = forward_transform(merged(arrived))
    prod_re = first_re[:per_stream]
    prod_im = first_im[:per_stream]
    filt_re = first_re[per_stream:]
    filt_im = first_im[per_stream:]
    mixed_re = prod_re * filt_re - prod_im * filt_im
    mixed_im = prod_re * filt_im + prod_im * filt_re
    mixed_cols = inverse_transform(mixed_re, mixed_im, grid_rows).astype(jnp.bfloat16)
    mixed_back = regroup_back(mixed_cols.reshape(1, per_stream, grid_rows, mixed_cols.shape[2]))
    mixed = mixed_back[0].T.astype(jnp.float32)
    gated = (query_side * mixed).astype(jnp.bfloat16)
    upstream = cotangent.astype(jnp.float32)
    mixed_grad = (upstream * query_side).astype(jnp.bfloat16)
    query_grad = upstream * mixed
    grad_cols = regroup_out(mixed_grad.T[None])
    grad_re, grad_im = forward_transform(merged(grad_cols))
    through_re = filt_re * grad_re + filt_im * grad_im
    through_im = filt_re * grad_im - filt_im * grad_re
    lagged_re = prod_re * grad_re + prod_im * grad_im
    lagged_im = prod_re * grad_im - prod_im * grad_re
    both_times = inverse_transform(
        jnp.concatenate([through_re, lagged_re], axis=0),
        jnp.concatenate([through_im, lagged_im], axis=0),
        grid_rows,
    )
    product_grad_cols = both_times[:per_stream].astype(jnp.bfloat16)
    filter_grad_cols = (both_times[per_stream:] * scale_factor).astype(jnp.bfloat16)
    returned = regroup_back(jnp.stack([product_grad_cols, filter_grad_cols]))
    product_grad = returned[0].T.astype(jnp.float32)
    filter_grad = returned[1].T
    conv_grad = jnp.stack([query_grad, product_grad * value_side, product_grad * key_side])
    following = shifted(conv_grad[:, :tap_reach, :].astype(jnp.bfloat16), "ctx", -1).astype(
        jnp.float32
    )
    extended_grad = jnp.concatenate([conv_grad, following], axis=1)
    running = jnp.zeros((3, block_rows, streams.shape[2]), jnp.float32)
    for offset in range(tap_reach + 1):
        running = (
            running + taps[:, offset, None, :] * extended_grad[:, offset : offset + block_rows, :]
        )
    stream_grad = running.astype(jnp.bfloat16)
    tap_terms = jnp.stack(
        [
            jnp.sum(
                conv_grad * extended[:, tap_reach - offset : tap_reach - offset + block_rows, :],
                axis=1,
            )
            for offset in range(tap_reach + 1)
        ],
        axis=1,
    )
    tap_grad = lax.psum(tap_terms, "ctx") * scale_factor
    return (gated, stream_grad, filter_grad, tap_grad)


def local(streams, taps, filters, cotangent):
    count = lax.axis_size("ctx")
    rows, channels = filters.shape
    tap_count = taps.shape[1]
    pairs_fill_lanes = channels == count * HALF and count % 2 == 0
    short_enough = rows % LANES == 0 and 3 * (rows * count) ** 2 <= TABLE_BYTES and tap_count < EDGE
    if pairs_fill_lanes and short_enough:
        return local_dense(streams, taps, filters, cotangent)
    return local_factored(streams, taps, filters, cotangent)


def solution(mesh):
    in_specs = (P(None, "ctx", "fft"), P(None, None, "fft"), P("ctx", "fft"), P("ctx", "fft"))
    out_specs = (P("ctx", "fft"), P(None, "ctx", "fft"), P("ctx", "fft"), P(None, None, "fft"))
    return jax.shard_map(local, mesh=mesh, in_specs=in_specs, out_specs=out_specs, check_vma=False)
```
